256 devices in a mesh: seq: 64 (over z, x, core), head: 4 (over y).
Axes of the slice: x: 4, y: 4, z: 8, core: 2. Of those that a mesh axis runs over, the one named last changes fastest.
Arguments:
- video_q: bfloat16 [8192, 2048], P('seq', 'head'), may hold values from -7.5 to 7.5
- video_k: bfloat16 [8192, 2048], P('seq', 'head'), may hold values from -7.5 to 7.5
- video_v: bfloat16 [8192, 2048], P('seq', 'head'), may hold values from -24 to 24
- audio_q: bfloat16 [512, 2048], P('seq', 'head'), may hold values from -7.5 to 7.5
- audio_k: bfloat16 [512, 2048], P('seq', 'head'), may hold values from -7.5 to 7.5
- audio_v: bfloat16 [512, 2048], P('seq', 'head'), may hold values from -24 to 24
- video_lengths: int32 [4], replicated, may hold values from 1 to 3584, 8192 in all
- audio_lengths: int32 [4], replicated, may hold values from 1 to 224, 512 in all
- video_out_weight: bfloat16 [2048, 4096], P(None, 'head'), may hold values from -0.125 to 0.125
- audio_out_weight: bfloat16 [2048, 2048], P(None, 'head'), may hold values from -0.125 to 0.125
Outputs:
- video_out: bfloat16 [8192, 4096], P('seq', 'head')
- audio_out: bfloat16 [512, 2048], P('seq', 'head')
The draws below stay inside these ranges and needn't reach their ends.
Inputs may be any that keep to these rules, and one draw needn't show every extreme that they name: `video_lengths`: clips lie end to end in order; one clip has exactly 3584 video tokens. `audio_lengths`: clips lie end to end in order; one clip has exactly 224 audio tokens.
All inputs are finite; a program needn't handle non-finite values.
Results may differ from the reference program's by a relative error of at most 0.012.
Values may be sent and summed in bfloat16 or wider, within the bound.
A program may use at most 64 MiB of HBM per device.

```python
import math
import jax
import jax.numpy as jnp
import numpy as np
from jax import lax

DV = 4096
DA = 2048
HEADS = 32
HEAD_DIM = 64
CLIPS = 4
INNER = 2048
VTOKENS = 8192
ATOKENS = 512
VMOST = 3584
AMOST = 224


def drawn_draw(key, row_count, salt):
    drawn = jax.random.normal(jax.random.fold_in(key, salt), (row_count, INNER), jnp.float32)
    return jnp.clip(drawn, -7.5, 7.5)


def draw_video_q(key, part):
    return drawn_draw(key, VTOKENS, 11).astype(jnp.bfloat16)


def draw_video_k(key, part):
    return drawn_draw(key, VTOKENS, 21).astype(jnp.bfloat16)


def draw_audio_q(key, part):
    return drawn_draw(key, ATOKENS, 31).astype(jnp.bfloat16)


def draw_audio_k(key, part):
    return drawn_draw(key, ATOKENS, 41).astype(jnp.bfloat16)


def level_of(key, shape, pieces, least, largest):
    factor_of, own = 1.0, jax.random.fold_in(key, 6)
    for dim, parts in pieces:
        steps = jnp.exp(jax.random.uniform(jax.random.fold_in(own, dim), (parts,), jnp.float32, least / len(pieces), largest / len(pieces)))
        factor_of = factor_of * jnp.repeat(steps, shape[dim] // parts).reshape([-1 if axis == dim else 1 for axis in range(len(shape))])
    return factor_of


def length_profile(number_of, total, reach, lean):
    loads = [(1 << 20) // math.isqrt(grade ** lean) + 1 for grade in range(2, number_of + 1)]
    rest, holding = total - reach - (number_of - 1), [1] * (number_of - 1)
    while rest > 0:
        movable = [i for i in range(number_of - 1) if holding[i] < reach]
        pool, budget = sum([loads[i] for i in movable]), rest
        for i in movable:
            extra = min(reach - holding[i], max(1, budget * loads[i] // pool), rest)
            holding[i] = holding[i] + extra
            rest = rest - extra
    return np.array([reach] + holding)


def uneven(own_key, amount, total, reach, lean):
    if amount == 2:
        one = jax.random.randint(own_key, (), max(1, total - reach), min(reach, total - 1) + 1)
        return jnp.stack([one, total - one])
    sizes = jnp.asarray(length_profile(amount, total, reach, lean), jnp.int32)
    twos = (amount - 1) // 2
    source_of, taker = sizes[1:1 + 2 * twos:2], sizes[2:2 + 2 * twos:2]
    margin = jnp.minimum(source_of - 1, reach - taker)
    moved = jax.random.randint(jax.random.fold_in(own_key, 1), (twos,), 0, 1 << 20) % (margin + 1)
    sizes = sizes.at[1:1 + 2 * twos:2].set(source_of - moved).at[2:2 + 2 * twos:2].set(taker + moved)
    return sizes[jax.random.permutation(jax.random.fold_in(own_key, 2), amount)]


def bell_draw(stream_key, shape, scale, limit, split=(), kind=jnp.bfloat16):
    array = scale * jax.random.normal(stream_key, shape, jnp.float32)
    if split:
        array = array * level_of(stream_key, shape, split, -0.22, 0.18)
    return jnp.clip(array, -limit, limit).astype(kind)


def setup_inputs(seed: int = 0) -> dict:
    streams_of = jax.random.split(jax.random.key(seed), 11)
    video_q = draw_video_q(jax.random.fold_in(streams_of[10], 71), 0)
    video_k = draw_video_k(jax.random.fold_in(streams_of[10], 71), 0)
    video_v = bell_draw(streams_of[2], (VTOKENS, INNER), 4.0, 24.0, ((0, 64), (1, 4)))
    audio_q = draw_audio_q(jax.random.fold_in(streams_of[10], 71), 0)
    audio_k = draw_audio_k(jax.random.fold_in(streams_of[10], 71), 0)
    audio_v = bell_draw(streams_of[5], (ATOKENS, INNER), 4.0, 24.0, ((0, 64), (1, 4)))
    video_lengths = uneven(streams_of[6], CLIPS, VTOKENS, VMOST, 2).astype(jnp.int32)
    audio_lengths = uneven(streams_of[7], CLIPS, ATOKENS, AMOST, 2).astype(jnp.int32)
    video_out_weight = bell_draw(streams_of[8], (INNER, DV), INNER ** -0.5, 0.125, ((1, 4),))
    audio_out_weight = bell_draw(streams_of[9], (INNER, DA), INNER ** -0.5, 0.125, ((1, 4),))
    return dict(video_q=video_q, video_k=video_k, video_v=video_v, audio_q=audio_q, audio_k=audio_k, audio_v=audio_v, video_lengths=video_lengths, audio_lengths=audio_lengths, video_out_weight=video_out_weight, audio_out_weight=audio_out_weight)


masked_floor = -1e+30

def clip_index(positions, lengths):
    clip_ends = jnp.cumsum(lengths).astype(jnp.int32)
    return lax.optimization_barrier(jnp.sum((positions[:, None] >= clip_ends[None, :]).astype(jnp.int32), axis=1)).astype(jnp.int32)

def attend_block(query, query_clip, key_heads, value_heads, key_clip):
    query_heads = query.astype(jnp.float32).reshape(query.shape[0], HEADS, HEAD_DIM)
    scores = jnp.einsum('qhd,khd->qhk', query_heads, key_heads, precision=lax.Precision.HIGHEST) / math.sqrt(HEAD_DIM)
    allowed = query_clip[:, None, None] == key_clip[None, None, :]
    scores = jnp.where(allowed, scores, masked_floor)
    row_max = lax.optimization_barrier(jnp.max(scores, axis=2, keepdims=True))
    weights = jnp.where(allowed, jnp.exp(scores - row_max), 0.0)
    totals = lax.optimization_barrier(jnp.sum(weights, axis=2))
    rounded = lax.optimization_barrier(weights.astype(jnp.bfloat16)).astype(jnp.float32)
    weighted = jnp.einsum('qhk,khd->qhd', rounded, value_heads, precision=lax.Precision.HIGHEST)
    return (weighted / totals[:, :, None]).reshape(query.shape[0], INNER).astype(jnp.bfloat16)

def reference(video_q, video_k, video_v, audio_q, audio_k, audio_v, video_lengths, audio_lengths, video_out_weight, audio_out_weight):
    video_clip = clip_index(jnp.arange(VTOKENS, dtype=jnp.int32), video_lengths)
    audio_pos = ((jnp.arange(ATOKENS, dtype=jnp.int32) + ATOKENS // 2) % ATOKENS).astype(jnp.int32)
    audio_clip = clip_index(audio_pos, audio_lengths)
    audio_keys = audio_k.astype(jnp.float32).reshape(ATOKENS, HEADS, HEAD_DIM)
    audio_values = audio_v.astype(jnp.float32).reshape(ATOKENS, HEADS, HEAD_DIM)
    video_keys = video_k.astype(jnp.float32).reshape(VTOKENS, HEADS, HEAD_DIM)
    video_values = video_v.astype(jnp.float32).reshape(VTOKENS, HEADS, HEAD_DIM)
    video_block = min(512, VTOKENS)
    video_attn = lax.map(lambda paired: attend_block(paired[0], paired[1], audio_keys, audio_values, audio_clip), (video_q.reshape(VTOKENS // video_block, video_block, INNER), video_clip.reshape(VTOKENS // video_block, video_block))).reshape(VTOKENS, INNER)
    audio_block = min(32, ATOKENS)
    audio_attn = lax.map(lambda paired: attend_block(paired[0], paired[1], video_keys, video_values, video_clip), (audio_q.reshape(ATOKENS // audio_block, audio_block, INNER), audio_clip.reshape(ATOKENS // audio_block, audio_block))).reshape(ATOKENS, INNER)
    video_out = jnp.dot(video_attn, video_out_weight, preferred_element_type=jnp.float32).astype(jnp.bfloat16)
    audio_out = jnp.dot(audio_attn, audio_out_weight, preferred_element_type=jnp.float32).astype(jnp.bfloat16)
    return (video_out, audio_out)
```

```python
import math

import jax
import jax.numpy as jnp
from jax import lax
from jax.experimental import pallas as pl
from jax.experimental.pallas import tpu as pltpu
from jax.sharding import PartitionSpec as P

HEAD_DIM = 64
GROUP = 8
MESH = pl.DeviceIdType.MESH
BF = jnp.bfloat16
F32 = jnp.float32
FORBID = -65536.0
LOG2E = math.log2(math.e)
SCALE = LOG2E / math.sqrt(HEAD_DIM)


def nt_dot(a, b):
    return lax.dot_general(a, b, (((1,), (1,)), ((), ())), preferred_element_type=F32)


def nn_dot(a, b):
    return lax.dot_general(a, b, (((1,), (0,)), ((), ())), preferred_element_type=F32)


def swap(x):
    return pltpu.roll(x, 64, x.ndim - 1)


def kernel(
    nz, ny,
    vl, al, vq, vk, vv, aq, ak, av, wv_hbm, wa_hbm,
    vo, ao,
    inq, ink, inv, ina_q, ina_k, ina_v, wv, wa,
    tok_aug, aud_aug,
    sendq, sendkv, senda, recvq, recvkv, recva,
    zkv, zq, kk, v0, v1,
    sendo, recvo, sendr, recvr, sendf, recvf, attn, aud,
    in_sem,
    q_s, q_r, kv_s, kv_r, a_s, a_r, zk_s, zk_r, zq_s, zq_r, r_s, r_r, o_s, o_r, f_s, f_r,
):
    s = lax.axis_index("seq")
    y = lax.axis_index("head")
    z = s // GROUP
    j = lax.rem(s, GROUP)
    at = nz * 64

    def loop(lo, hi, body):
        def step(i, carry):
            body(i)
            return carry
        lax.fori_loop(lo, hi, step, 0)

    def in_group(d):
        return lax.rem(j + d, GROUP)

    def in_ring(d):
        return lax.rem(z + d, nz)

    def peer(zz, jj, yy):
        return (zz * GROUP + jj, yy)

    def remote(src, dst, ss, rs, to):
        return pltpu.make_async_remote_copy(
            src_ref=src, dst_ref=dst, send_sem=ss, recv_sem=rs, device_id=to, device_id_type=MESH
        )

    local = [
        pltpu.make_async_copy(src, dst, in_sem.at[i])
        for i, (src, dst) in enumerate(
            [(aq, ina_q), (ak, ina_k), (av, ina_v), (vq, inq), (vk, ink), (vv, inv), (wv_hbm, wv), (wa_hbm, wa)]
        )
    ]
    for c in local:
        c.start()

    barrier = pltpu.get_barrier_semaphore()

    def greet_out(i):
        n = i + 1
        pl.semaphore_signal(
            barrier, inc=1,
            device_id=peer(z, lax.rem(j + lax.rem(n, GROUP), GROUP), lax.rem(y + n // GROUP, ny)),
            device_id_type=MESH,
        )

    loop(0, GROUP * ny - 1, greet_out)

    def greet_ring(d):
        pl.semaphore_signal(barrier, inc=1, device_id=peer(in_ring(d), j, y), device_id_type=MESH)

    loop(1, nz, greet_ring)

    v_end = [vl[0]]
    a_end = [al[0]]
    for c in range(1, 4):
        v_end.append(v_end[-1] + vl[c])
        a_end.append(a_end[-1] + al[c])

    def clip_of(pos, ends):
        total = jnp.zeros_like(pos)
        for e in ends:
            total = total + (pos >= e).astype(jnp.int32)
        return total

    blk = lax.broadcasted_iota(jnp.int32, (GROUP, 64, 128), 0)
    row = lax.broadcasted_iota(jnp.int32, (GROUP, 64, 128), 1)
    lane = lax.broadcasted_iota(jnp.int32, (GROUP, 64, 128), 2)
    token = (z * GROUP + blk) * 128 + row + jnp.where(lane < 4, 0, 64)
    mark = jnp.where(lane < 4, lane, lane - 4)
    one_hot = (lane < 8) & (clip_of(token, v_end) == mark)
    tok_aug[...] = jnp.where(one_hot, 1.0, 0.0).astype(BF)

    blk = lax.broadcasted_iota(jnp.int32, (nz, 64, 128), 0)
    row = lax.broadcasted_iota(jnp.int32, (nz, 64, 128), 1)
    lane = lax.broadcasted_iota(jnp.int32, (nz, 64, 128), 2)
    pos = blk * 64 + row + at // 2
    pos = jnp.where(pos >= at, pos - at, pos)
    a_clip = clip_of(pos, a_end)
    aud_aug[0] = jnp.where((lane < 4) & (a_clip != lane), FORBID, 0.0).astype(BF)
    aud_aug[1] = jnp.where((lane >= 4) & (lane < 8) & (a_clip != lane - 4), FORBID, 0.0).astype(BF)

    def low(shape):
        return lax.broadcasted_iota(jnp.int32, shape, len(shape) - 1) < 64

    for i in range(3):
        local[i].wait()
    low8 = low((8, 128))
    for p in range(4):
        cols = pl.ds(128 * p, 128)
        q8, k8, v8 = (r[:, cols].astype(F32) for r in (ina_q, ina_k, ina_v))
        even = jnp.concatenate([jnp.where(low8, k8, swap(v8)), q8], axis=0)
        odd = jnp.concatenate([jnp.where(low8, swap(k8), v8), swap(q8)], axis=0)
        senda[2 * p] = even.astype(BF)
        senda[2 * p + 1] = odd.astype(BF)

    low64 = low((64, 128))

    def halves(ref, put):
        for p in range(4):
            cols = pl.ds(128 * p, 128)
            top = ref[0:64, cols].astype(F32)
            bottom = ref[64:128, cols].astype(F32)
            put(2 * p, jnp.where(low64, top, swap(bottom)).astype(BF))
            put(2 * p + 1, jnp.where(low64, swap(top), bottom).astype(BF))

    def put_q(h, x):
        sendq[h] = x

    def put_k(h, x):
        sendkv[h, 0] = x

    def put_v(h, x):
        sendkv[h, 1] = x

    local[3].wait()
    halves(inq, put_q)

    pl.semaphore_wait(barrier, GROUP * ny - 1 + nz - 1)

    def a_copy(t):
        return remote(senda.at[t], recva.at[j], a_s.at[t], a_r.at[j], peer(z, t, y))

    def q_copy(t):
        return remote(sendq.at[t], recvq.at[j], q_s.at[t], q_r.at[j], peer(z, t, y))

    def kv_copy(t):
        return remote(sendkv.at[t], recvkv.at[j], kv_s.at[t], kv_r.at[j], peer(z, t, y))

    def arrived(dst, rs):
        remote(dst, dst, rs, rs, peer(z, in_group(1), y)).wait_recv()

    loop(1, GROUP, lambda d: a_copy(in_group(d)).start())
    loop(1, GROUP, lambda d: q_copy(in_group(d)).start())
    local[4].wait()
    halves(ink, put_k)
    local[5].wait()
    halves(inv, put_v)
    loop(1, GROUP, lambda d: kv_copy(in_group(d)).start())
    recva[j] = senda[j]
    recvq[j] = sendq[j]
    recvkv[j] = sendkv[j]

    def wait_a(d):
        t = in_group(d)
        arrived(recva.at[t], a_r.at[t])

    loop(1, GROUP, wait_a)
    got = recva[...].astype(F32)
    zkv[z] = got[:, 0:8, :].reshape(64, 128).astype(BF)
    q64 = got[:, 8:16, :].reshape(64, 128)
    zq[z] = jnp.where(low((32, 128)), q64[0:32], swap(q64[32:64])).astype(BF)

    def zk_copy(d):
        t = in_ring(d)
        return remote(zkv.at[z], zkv.at[z], zk_s.at[t], zk_r.at[z], peer(t, j, y))

    def zq_copy(d):
        t = in_ring(d)
        return remote(zq.at[z], zq.at[z], zq_s.at[t], zq_r.at[z], peer(t, j, y))

    loop(1, nz, lambda d: zk_copy(d).start())
    loop(1, nz, lambda d: zq_copy(d).start())

    def wait_zk(d):
        t = in_ring(d)
        arrived(zkv.at[t], zk_r.at[t])

    loop(1, nz, wait_zk)
    kv = zkv[...].reshape(at, 128).astype(F32)
    vk_ = swap(kv)
    low_at = low((at, 128))
    kk[0:at] = jnp.where(low_at, kv, 0.0).astype(BF)
    kk[at : 2 * at] = jnp.where(low_at, 0.0, vk_).astype(BF)
    v0[...] = jnp.where(low_at, vk_, 1.0).astype(BF)
    v1[...] = jnp.where(low_at, 1.0, kv).astype(BF)

    def wait_q(d):
        t = in_group(d)
        arrived(recvq.at[t], q_r.at[t])

    loop(1, GROUP, wait_q)

    def o_copy(t, e):
        u = lax.rem(y + e, ny)
        return remote(sendo.at[t], recvo.at[y, j], o_s.at[u, t], o_r.at[y, j], peer(z, t, u))

    def video_block(t):
        query = jnp.concatenate([recvq[t], tok_aug[t]], axis=1)
        keys = jnp.concatenate([kk[0 : 2 * at], aud_aug[...].reshape(2 * at, 128)], axis=1)
        sc = nt_dot(query, keys)
        outs = []
        for half, values in ((sc[:, 0:at], v0), (sc[:, at : 2 * at], v1)):
            top = jnp.max(half, axis=1, keepdims=True)
            w = jnp.exp2((half - top) * SCALE).astype(BF)
            outs.append(nn_dot(w, values[...]))
        num = jnp.where(low64, outs[0], outs[1])
        den = swap(jnp.where(low64, outs[1], outs[0]))
        return (num / den).astype(BF)

    def video_step(d):
        t = in_group(d)
        sendo[t] = video_block(t)
        loop(0, ny, lambda e: o_copy(t, e).start())

    loop(1, GROUP, video_step)
    sendo[j] = video_block(j)
    loop(1, ny, lambda e: o_copy(j, e).start())
    recvo[y, j] = sendo[j]

    def wait_kv(d):
        t = in_group(d)
        arrived(recvkv.at[t], kv_r.at[t])

    loop(1, GROUP, wait_kv)

    def wait_zq(d):
        t = in_ring(d)
        arrived(zq.at[t], zq_r.at[t])

    loop(1, nz, wait_zq)
    low_gt = low((GROUP * 64, 128))
    vp = recvkv[:, 1].reshape(GROUP * 64, 128).astype(F32)
    v0g = jnp.where(low_gt, vp, 1.0).astype(BF)
    v1g = jnp.where(low_gt, 1.0, vp).astype(BF)
    kk[0 : GROUP * 64] = v0g
    kk[GROUP * 64 : 2 * GROUP * 64] = v1g
    low32 = low((32, 128))
    lane64 = lax.broadcasted_iota(jnp.int32, (64, 128), 1)

    def audio_block(t):
        qp = zq[t].astype(F32)
        qs = swap(qp)
        query = jnp.concatenate(
            [
                jnp.where(low32, qp, 0.0), jnp.where(low32, qs, 0.0),
                jnp.where(low32, 0.0, qs), jnp.where(low32, 0.0, qp),
            ],
            axis=0,
        ).astype(BF)
        query = jnp.concatenate([query, aud_aug[:, t].reshape(128, 128)], axis=1)
        keys = jnp.concatenate(
            [recvkv[:, 0].reshape(GROUP * 64, 128), tok_aug[...].reshape(GROUP * 64, 128)], axis=1
        )
        sc = nt_dot(query, keys)
        top = jnp.max(sc, axis=1, keepdims=True)
        top = jnp.maximum(top[0:64], top[64:128])
        w0 = jnp.exp2((sc[0:64] - top) * SCALE).astype(BF)
        w1 = jnp.exp2((sc[64:128] - top) * SCALE).astype(BF)
        full = nn_dot(w0, kk[0 : GROUP * 64]) + swap(nn_dot(w1, kk[GROUP * 64 : 2 * GROUP * 64]))
        mean = full / swap(full)
        level = top * SCALE + jnp.log(jnp.where(low64, 1.0, full)) * LOG2E
        first = level.astype(BF).astype(F32)
        second = (level - first).astype(BF).astype(F32)
        third = level - first - second
        parts = jnp.where(lane64 < 96, first, jnp.where(lane64 < 112, second, third))
        return jnp.where(low64, mean, parts).astype(BF)

    def r_copy(d):
        t = in_ring(d)
        return remote(sendr.at[t], recvr.at[z], r_s.at[t], r_r.at[z], peer(t, j, y))

    def audio_step(d):
        t = in_ring(d)
        sendr[t] = audio_block(t)
        r_copy(d).start()

    loop(1, nz, audio_step)
    recvr[z] = audio_block(z)

    def wait_r(d):
        t = in_ring(d)
        arrived(recvr.at[t], r_r.at[t])

    loop(1, nz, wait_r)
    part = recvr[...].astype(F32)
    level = part[:, :, 64:65] + part[:, :, 96:97] + part[:, :, 112:113]
    share = jnp.exp2(level - jnp.max(level, axis=0, keepdims=True))
    mixed = jnp.sum(part * share, axis=0) / jnp.sum(share, axis=0)
    sendf[...] = mixed.reshape(GROUP, 8, 128)

    def f_copy(n):
        t = lax.rem(j + lax.rem(n, GROUP), GROUP)
        u = lax.rem(y + n // GROUP, ny)
        return remote(sendf.at[t], recvf.at[y, j], f_s.at[u, t], f_r.at[y, j], peer(z, t, u))

    loop(1, GROUP * ny, lambda n: f_copy(n).start())
    recvf[y, j] = sendf[j]

    def wait_o(n):
        t = lax.rem(j + lax.rem(n, GROUP), GROUP)
        u = lax.rem(y + n // GROUP, ny)
        arrived(recvo.at[u, t], o_r.at[u, t])

    loop(1, GROUP * ny, wait_o)
    for u in range(ny):
        for x in range(GROUP // 2):
            cols = pl.ds((u * 4 + x) * 128, 128)
            a0 = recvo[u, 2 * x].astype(F32)
            a1 = recvo[u, 2 * x + 1].astype(F32)
            attn[0:64, cols] = jnp.where(low64, a0, swap(a1)).astype(BF)
            attn[64:128, cols] = jnp.where(low64, swap(a0), a1).astype(BF)
    local[6].wait()
    width = wv.shape[1] // 4
    for n in range(4):
        cols = pl.ds(n * width, width)
        vo[:, cols] = nn_dot(attn[...], wv[:, cols]).astype(BF)

    def wait_f(n):
        t = lax.rem(j + lax.rem(n, GROUP), GROUP)
        u = lax.rem(y + n // GROUP, ny)
        arrived(recvf.at[u, t], f_r.at[u, t])

    loop(1, GROUP * ny, wait_f)
    for u in range(ny):
        for x in range(GROUP // 2):
            cols = pl.ds((u * 4 + x) * 128, 128)
            aud[:, cols] = jnp.where(low8, recvf[u, 2 * x], swap(recvf[u, 2 * x + 1]))
    local[7].wait()
    ao[...] = nn_dot(aud[...].astype(BF), wa[...]).astype(BF)

    def sent_group(d):
        t = in_group(d)
        a_copy(t).wait_send()
        q_copy(t).wait_send()
        kv_copy(t).wait_send()

    def sent_ring(d):
        zk_copy(d).wait_send()
        zq_copy(d).wait_send()
        r_copy(d).wait_send()

    def sent_out(n):
        t = lax.rem(j + lax.rem(n, GROUP), GROUP)
        o_copy(t, n // GROUP).wait_send()
        f_copy(n).wait_send()

    loop(1, GROUP, sent_group)
    loop(1, nz, sent_ring)
    loop(1, GROUP * ny, sent_out)


def per_device(nz, ny, vq, vk, vv, aq, ak, av, vl, al, wv, wa):
    rows, width = vq.shape
    a_rows = aq.shape[0]
    at = nz * 64
    hbm = pl.BlockSpec(memory_space=pl.ANY)
    smem = pl.BlockSpec(memory_space=pltpu.SMEM)
    vmem = pl.BlockSpec(memory_space=pltpu.VMEM)
    bf = lambda *shape: pltpu.VMEM(shape, BF)
    dma = lambda *shape: pltpu.SemaphoreType.DMA(shape)

    def body(*refs):
        kernel(nz, ny, *refs)

    return pl.pallas_call(
        body,
        out_shape=(
            jax.ShapeDtypeStruct((rows, wv.shape[1]), BF),
            jax.ShapeDtypeStruct((a_rows, wa.shape[1]), BF),
        ),
        in_specs=[smem, smem] + [hbm] * 8,
        out_specs=(vmem, vmem),
        scratch_shapes=[
            bf(rows, width), bf(rows, width), bf(rows, width),
            bf(a_rows, width), bf(a_rows, width), bf(a_rows, width),
            bf(*wv.shape), bf(*wa.shape),
            bf(GROUP, 64, 128), bf(2, nz, 64, 128),
            bf(GROUP, 64, 128), bf(GROUP, 2, 64, 128), bf(GROUP, 16, 128),
            bf(GROUP, 64, 128), bf(GROUP, 2, 64, 128), bf(GROUP, 16, 128),
            bf(nz, 64, 128), bf(nz, 32, 128),
            bf(2 * max(at, GROUP * 64), 128), bf(at, 128), bf(at, 128),
            bf(GROUP, 64, 128), bf(ny, GROUP, 64, 128),
            bf(nz, 64, 128), bf(nz, 64, 128),
            pltpu.VMEM((GROUP, 8, 128), F32), pltpu.VMEM((ny, GROUP, 8, 128), F32),
            bf(rows, ny * width), pltpu.VMEM((a_rows, ny * width), F32),
            dma(8),
            dma(GROUP), dma(GROUP), dma(GROUP), dma(GROUP), dma(GROUP), dma(GROUP),
            dma(nz), dma(nz), dma(nz), dma(nz), dma(nz), dma(nz),
            dma(ny, GROUP), dma(ny, GROUP), dma(ny, GROUP), dma(ny, GROUP),
        ],
        compiler_params=pltpu.CompilerParams(
            collective_id=0, has_side_effects=True, vmem_limit_bytes=56 * 1024 * 1024
        ),
        name="cross_attention",
    )(vl, al, vq, vk, vv, aq, ak, av, wv, wa)


def solution(mesh):
    nz = mesh.shape["seq"] // GROUP
    ny = mesh.shape["head"]

    def program(*arrays):
        return per_device(nz, ny, *arrays)

    return jax.shard_map(
        program,
        mesh=mesh,
        in_specs=(*(P("seq", "head"),) * 6, P(), P(), P(None, "head"), P(None, "head")),
        out_specs=(P("seq", "head"), P("seq", "head")),
        check_vma=False,
    )
```

```python
import math

import jax
import jax.numpy as jnp
from jax import lax
from jax.experimental import pallas as pl
from jax.experimental.pallas import tpu as pltpu
from jax.sharding import PartitionSpec as P

HEAD_DIM = 64
NX = 4
MESH = pl.DeviceIdType.MESH
BF = jnp.bfloat16
F32 = jnp.float32
FORBID = -65536.0
LOG2E = math.log2(math.e)
SCALE = LOG2E / math.sqrt(HEAD_DIM)


def nt_dot(a, b):
    return lax.dot_general(a, b, (((1,), (1,)), ((), ())), preferred_element_type=F32)


def nn_dot(a, b):
    return lax.dot_general(a, b, (((1,), (0,)), ((), ())), preferred_element_type=F32)


def swap(x):
    return pltpu.roll(x, 64, x.ndim - 1)


def lanes(shape):
    return lax.broadcasted_iota(jnp.int32, shape, len(shape) - 1)


def low(shape):
    return lanes(shape) < 64


def kernel(
    nz, ny,
    vl, al, vq, vk, vv, aq, ak, av, wv_hbm, wa_hbm,
    vo, ao,
    ina_q, ina_k, ina_v, wv, wa,
    tok_aug, aud_aug,
    senda, recva, recvq, kvb, zkv, zq, kk, v0, v1,
    sendo, attn, sendr, recvr, sendx, recvx, sendf, aud,
    in_sem,
    a_s, a_r, q_s, q_r, kv_s, kv_r, zk_s, zk_r, zq_s, zq_r, c_s, c_r, r_s, r_r, o_s, o_r, f_s, f_r,
):
    s = lax.axis_index("seq")
    y = lax.axis_index("head")
    z = s // (2 * NX)
    x = lax.rem(s // 2, NX)
    c = lax.rem(s, 2)
    other = 1 - c
    at = nz * 64
    vt = 2 * NX * 128

    def loop(lo, hi, body):
        def step(i, carry):
            body(i)
            return carry
        lax.fori_loop(lo, hi, step, 0)

    def at_x(d):
        return lax.rem(x + d, NX)

    def at_z(d):
        return lax.rem(z + d, nz)

    def at_y(d):
        return lax.rem(y + d, ny)

    def peer(zz, xx, cc, yy):
        return ((zz * NX + xx) * 2 + cc, yy)

    def remote(src, dst, ss, rs, to):
        return pltpu.make_async_remote_copy(
            src_ref=src, dst_ref=dst, send_sem=ss, recv_sem=rs, device_id=to, device_id_type=MESH
        )

    partner = peer(z, x, other, y)

    def arrived(dst, rs):
        remote(dst, dst, rs, rs, partner).wait_recv()

    def columns(ref, t):
        return ref.at[:, pl.ds(pl.multiple_of(t * 128, 128), 128)]

    local = [
        pltpu.make_async_copy(src, dst, in_sem.at[i])
        for i, (src, dst) in enumerate(
            [
                (aq, ina_q), (ak, ina_k), (av, ina_v),
                (columns(vq, x), recvq.at[x]),
                (columns(vk, x), kvb.at[c, x, 0]),
                (columns(vv, x), kvb.at[c, x, 1]),
                (wv_hbm, wv), (wa_hbm, wa),
            ]
        )
    ]
    for copy in local:
        copy.start()

    barrier = pltpu.get_barrier_semaphore()

    def greet(to):
        pl.semaphore_signal(barrier, inc=1, device_id=to, device_id_type=MESH)

    greet(partner)
    loop(1, nz, lambda d: greet(peer(at_z(d), x, c, y)))
    loop(1, NX * ny, lambda n: greet(peer(z, at_x(lax.rem(n, NX)), c, at_y(n // NX))))

    v_end = [vl[0]]
    a_end = [al[0]]
    for i in range(1, 4):
        v_end.append(v_end[-1] + vl[i])
        a_end.append(a_end[-1] + al[i])

    def clip_of(pos, ends):
        total = jnp.zeros_like(pos)
        for e in ends:
            total = total + (pos >= e).astype(jnp.int32)
        return total

    def iotas(shape):
        return [lax.broadcasted_iota(jnp.int32, shape, i) for i in range(len(shape))]

    core, place, row, lane = iotas((2, NX, 128, 128))
    token = ((z * NX + place) * 2 + core) * 128 + row
    tok_aug[...] = jnp.where(clip_of(token, v_end) == lane, 1.0, 0.0).astype(BF)
    core, slab, row, lane = iotas((2, nz, 32, 128))
    pos = slab * 64 + (row >> 3) * 16 + core * 8 + (row & 7) + at // 2
    pos = jnp.where(pos >= at, pos - at, pos)
    mark = jnp.where((lane < 4) & (clip_of(pos, a_end) != lane), FORBID, 0.0).astype(BF)
    aud_aug[...] = mark
    kk[0:at, 128:256] = mark.reshape(at, 128)
    kk[at : 2 * at, 128:256] = mark.reshape(at, 128)

    for i in range(3):
        local[i].wait()
    for p in range(NX):
        cols = pl.ds(128 * p, 128)
        k8, v8, q8 = (r[:, cols].astype(F32) for r in (ina_k, ina_v, ina_q))
        senda[p] = jnp.concatenate([k8, v8, q8, q8], axis=0).astype(BF)

    pl.semaphore_wait(barrier, 1 + nz - 1 + NX * ny - 1)

    def a_copy(d):
        t = at_x(d)
        return remote(senda.at[t], recva.at[x], a_s.at[t], a_r.at[x], peer(z, t, c, y))

    def q_copy(d):
        t = at_x(d)
        return remote(columns(vq, t), recvq.at[x], q_s.at[t], q_r.at[x], peer(z, t, c, y))

    def k_copy(d):
        t = at_x(d)
        return remote(columns(vk, t), kvb.at[c, x, 0], kv_s.at[0, t], kv_r.at[0, x], peer(z, t, c, y))

    def v_copy(d):
        t = at_x(d)
        return remote(columns(vv, t), kvb.at[c, x, 1], kv_s.at[1, t], kv_r.at[1, x], peer(z, t, c, y))

    for copy in (a_copy, q_copy, k_copy, v_copy):
        for d in range(1, NX):
            copy(d).start()

    recva[x] = senda[x]

    for d in range(1, NX):
        arrived(recva.at[at_x(d)], a_r.at[at_x(d)])
    got = recva[...].astype(F32)
    zkv[c, z] = jnp.concatenate([got[:, 0:8].reshape(32, 128), got[:, 8:16].reshape(32, 128)], axis=0).astype(BF)
    zq[c, z] = got[:, 16:24].reshape(32, 128).astype(BF)

    def zk_copy(d):
        t = at_z(d)
        return remote(zkv.at[c, z], zkv.at[c, z], zk_s.at[t], zk_r.at[z], peer(t, x, c, y))

    def zq_copy(d):
        t = at_z(d)
        return remote(zq.at[c, z], zq.at[c, z], zq_s.at[t], zq_r.at[z], peer(t, x, c, y))

    loop(1, nz, lambda d: zk_copy(d).start())
    loop(1, nz, lambda d: zq_copy(d).start())
    loop(1, nz, lambda d: arrived(zkv.at[c, at_z(d)], zk_r.at[at_z(d)]))

    zk_share = remote(zkv.at[c], zkv.at[c], c_s.at[0], c_r.at[0], partner)
    zq_share = remote(zq.at[c], zq.at[c], c_s.at[1], c_r.at[1], partner)
    kv_share = remote(kvb.at[c], kvb.at[c], c_s.at[2], c_r.at[2], partner)
    zk_share.start()
    local[3].wait()
    for d in range(1, NX):
        arrived(recvq.at[at_x(d)], q_r.at[at_x(d)])
    arrived(zkv.at[other], c_r.at[0])

    low_at = low((at, 128))
    key = zkv[:, :, 0:32].reshape(at, 128).astype(F32)
    kk[0:at, 0:128] = jnp.where(low_at, key, 0.0).astype(BF)
    kk[at : 2 * at, 0:128] = jnp.where(low_at, 0.0, key).astype(BF)
    value = zkv[:, :, 32:64].reshape(at, 128).astype(F32)
    v0[0:at] = jnp.where(low_at, value, 1.0).astype(BF)
    v1[...] = jnp.where(low_at, 1.0, value).astype(BF)

    low128 = low((128, 128))

    def o_copy(t, e):
        u = at_y(e)
        return remote(sendo.at[t], attn.at[y, x], o_s.at[u, t], o_r.at[y, x], peer(z, t, c, u))

    def video_block(t):
        query = jnp.concatenate([recvq[t], tok_aug[c, t]], axis=1)
        sc = nt_dot(query, kk[...])
        outs = []
        for half, values in ((sc[:, 0:at], v0[0:at]), (sc[:, at : 2 * at], v1[...])):
            top = jnp.max(half, axis=1, keepdims=True)
            w = jnp.exp2((half - top) * SCALE).astype(BF)
            outs.append(nn_dot(w, values))
        num = jnp.where(low128, outs[0], outs[1])
        den = swap(jnp.where(low128, outs[1], outs[0]))
        return (num / den).astype(BF)

    for d in range(1, NX):
        t = at_x(d)
        sendo[t] = video_block(t)
        for e in range(ny):
            o_copy(t, e).start()
        if d == 2:
            for i in (4, 5):
                local[i].wait()
            for n in range(1, NX):
                for i in range(2):
                    arrived(kvb.at[c, at_x(n), i], kv_r.at[i, at_x(n)])
            kv_share.start()
            loop(1, nz, lambda n: arrived(zq.at[c, at_z(n)], zq_r.at[at_z(n)]))
            zq_share.start()
    sendo[x] = video_block(x)
    for e in range(1, ny):
        o_copy(x, e).start()
    attn[y, x] = sendo[x]

    arrived(kvb.at[other], c_r.at[2])
    arrived(zq.at[other], c_r.at[1])
    mine_vt = low((vt, 128)) == (c == 0)
    v0[0:vt] = jnp.where(mine_vt, kvb[:, :, 1].reshape(vt, 128).astype(F32), 1.0).astype(BF)
    mine128 = low128 == (c == 0)
    lane128 = lanes((128, 128))

    def audio_block(p):
        query = zq[:, pl.ds(2 * p, 2)].reshape(128, 128).astype(F32)
        query = jnp.where(mine128, query, 0.0).astype(BF)
        query = jnp.concatenate([query, aud_aug[:, pl.ds(2 * p, 2)].reshape(128, 128)], axis=1)
        keys = jnp.concatenate([kvb[:, :, 0].reshape(vt, 128), tok_aug[...].reshape(vt, 128)], axis=1)
        sc = nt_dot(query, keys)
        top = jnp.max(sc, axis=1, keepdims=True)
        w = jnp.exp2((sc - top) * SCALE).astype(BF)
        full = nn_dot(w, v0[0:vt])
        turned = swap(full)
        full, turned = jnp.where(c == 0, full, turned), jnp.where(c == 0, turned, full)
        mean = full / turned
        level = top * SCALE + jnp.log(jnp.where(low128, 1.0, full)) * LOG2E
        first = level.astype(BF).astype(F32)
        second = (level - first).astype(BF).astype(F32)
        third = level - first - second
        parts = jnp.where(lane128 < 96, first, jnp.where(lane128 < 112, second, third))
        out = jnp.where(low128, mean, parts).reshape(2, 2, 32, 128)
        return [out[:, i].reshape(64, 128).astype(BF) for i in range(2)]

    def r_copy(t):
        return remote(sendr.at[t], recvr.at[z], r_s.at[t], r_r.at[z], peer(t, x, c, y))

    def audio_step(d):
        p = lax.rem(z // 2 + d, nz // 2)
        done = audio_block(p)
        for i in range(2):
            sendr[2 * p + i] = done[i]
        for i in range(2):
            r_copy(2 * p + i).start()

    loop(1, nz // 2, audio_step)
    pair = z // 2
    near = 2 * pair + (1 - lax.rem(z, 2))
    done = audio_block(pair)
    for i in range(2):
        sendr[2 * pair + i] = done[i]
    r_copy(near).start()
    recvr[z] = sendr[z]

    loop(1, nz, lambda d: arrived(recvr.at[at_z(d)], r_r.at[at_z(d)]))
    part = recvr[...].astype(F32)
    level = part[:, :, 64:65] + part[:, :, 96:97] + part[:, :, 112:113]
    share = jnp.exp2(level - jnp.max(level, axis=0, keepdims=True))
    mixed = jnp.sum(part * share, axis=0) / jnp.sum(share, axis=0)
    mixed = jnp.where(c == 0, mixed, swap(mixed))
    sendx[...] = jnp.where(c == 0, mixed[32:64], mixed[0:32])
    x_share = remote(sendx, recvx, c_s.at[3], c_r.at[3], partner)
    x_share.start()
    arrived(recvx, c_r.at[3])
    mine32 = low((32, 128)) == (c == 0)
    both = jnp.where(mine32, jnp.where(c == 0, mixed[0:32], mixed[32:64]), recvx[...])
    sendf[...] = both.reshape(NX, 8, 128)

    def f_copy(n):
        t = at_x(lax.rem(n, NX))
        u = at_y(n // NX)
        return remote(sendf.at[t], aud.at[y, x], f_s.at[u, t], f_r.at[y, x], peer(z, t, c, u))

    loop(1, NX * ny, lambda n: f_copy(n).start())
    aud[y, x] = sendf[x]

    def wait_o(n):
        t = at_x(lax.rem(n, NX))
        u = at_y(n // NX)
        arrived(attn.at[u, t], o_r.at[u, t])

    loop(1, NX * ny, wait_o)
    every = [(u, t) for u in range(ny) for t in range(NX)]
    local[6].wait()
    hidden = jnp.concatenate([attn[u, t] for u, t in every], axis=1)
    width = wv.shape[1] // 4
    for n in range(4):
        cols = pl.ds(n * width, width)
        vo[:, cols] = nn_dot(hidden, wv[:, cols]).astype(BF)

    def wait_f(n):
        t = at_x(lax.rem(n, NX))
        u = at_y(n // NX)
        arrived(aud.at[u, t], f_r.at[u, t])

    loop(1, NX * ny, wait_f)
    local[7].wait()
    hidden = jnp.concatenate([aud[u, t] for u, t in every], axis=1).astype(BF)
    ao[...] = nn_dot(hidden, wa[...]).astype(BF)

    for copy in (a_copy, q_copy, k_copy, v_copy):
        for d in range(1, NX):
            copy(d).wait_send()
    for copy in (zk_share, zq_share, kv_share, x_share):
        copy.wait_send()

    def sent_ring(d):
        zk_copy(d).wait_send()
        zq_copy(d).wait_send()
        r_copy(at_z(d)).wait_send()

    def sent_out(n):
        o_copy(at_x(lax.rem(n, NX)), n // NX).wait_send()
        f_copy(n).wait_send()

    loop(1, nz, sent_ring)
    loop(1, NX * ny, sent_out)


def per_device(nz, ny, vq, vk, vv, aq, ak, av, vl, al, wv, wa):
    rows, width = vq.shape
    a_rows = aq.shape[0]
    at = nz * 64
    vt = 2 * NX * 128
    hbm = pl.BlockSpec(memory_space=pl.ANY)
    smem = pl.BlockSpec(memory_space=pltpu.SMEM)
    vmem = pl.BlockSpec(memory_space=pltpu.VMEM)
    bf = lambda *shape: pltpu.VMEM(shape, BF)
    wide = lambda *shape: pltpu.VMEM(shape, F32)
    dma = lambda *shape: pltpu.SemaphoreType.DMA(shape)

    def body(*refs):
        kernel(nz, ny, *refs)

    return pl.pallas_call(
        body,
        out_shape=(
            jax.ShapeDtypeStruct((rows, wv.shape[1]), BF),
            jax.ShapeDtypeStruct((a_rows, wa.shape[1]), BF),
        ),
        in_specs=[smem, smem] + [hbm] * 8,
        out_specs=(vmem, vmem),
        scratch_shapes=[
            bf(a_rows, width), bf(a_rows, width), bf(a_rows, width),
            bf(*wv.shape), bf(*wa.shape),
            bf(2, NX, 128, 128), bf(2, nz, 32, 128),
            bf(NX, 32, 128), bf(NX, 32, 128), bf(NX, 128, 128), bf(2, NX, 2, 128, 128),
            bf(2, nz, 64, 128), bf(2, nz, 32, 128),
            bf(2 * at, 256), bf(max(at, vt), 128), bf(at, 128),
            bf(NX, 128, 128), bf(ny, NX, 128, 128),
            bf(nz, 64, 128), bf(nz, 64, 128),
            wide(32, 128), wide(32, 128), wide(NX, 8, 128), wide(ny, NX, 8, 128),
            dma(8),
            dma(NX), dma(NX), dma(NX), dma(NX), dma(2, NX), dma(2, NX),
            dma(nz), dma(nz), dma(nz), dma(nz), dma(4), dma(4), dma(nz), dma(nz),
            dma(ny, NX), dma(ny, NX), dma(ny, NX), dma(ny, NX),
        ],
        compiler_params=pltpu.CompilerParams(
            collective_id=0, has_side_effects=True, vmem_limit_bytes=56 * 1024 * 1024
        ),
        name="cross_attention",
    )(vl, al, vq, vk, vv, aq, ak, av, wv, wa)


def solution(mesh):
    nz = mesh.shape["seq"] // (2 * NX)
    ny = mesh.shape["head"]

    def program(*arrays):
        return per_device(nz, ny, *arrays)

    return jax.shard_map(
        program,
        mesh=mesh,
        in_specs=(*(P("seq", "head"),) * 6, P(), P(), P(None, "head"), P(None, "head")),
        out_specs=(P("seq", "head"), P("seq", "head")),
        check_vma=False,
    )
```

```python
import math

import jax
import jax.numpy as jnp
from jax import lax
from jax.experimental import pallas as pl
from jax.experimental.pallas import tpu as pltpu
from jax.sharding import PartitionSpec as P

HEAD_DIM = 64
NX = 4
VIDEO = [[[1, 2]], [[3, 0]]]
AUDIO = 2
MESH = pl.DeviceIdType.MESH
BF = jnp.bfloat16
F32 = jnp.float32
FORBID = -65536.0
LOG2E = math.log2(math.e)
SCALE = LOG2E / math.sqrt(HEAD_DIM)


def nn_dot(a, b):
    return lax.dot_general(a, b, (((1,), (0,)), ((), ())), preferred_element_type=F32)


def swap(x):
    return pltpu.roll(x, 64, x.ndim - 1)


def lanes(shape):
    return lax.broadcasted_iota(jnp.int32, shape, len(shape) - 1)


def low(shape):
    return lanes(shape) < 64


def kernel(
    nz, ny,
    vl, al, vq, vk, vv, aq, ak, av, wv_hbm, wa_hbm,
    vo, ao,
    ina_q, ina_k, ina_v, wv, wa,
    tok_aug, aud_aug,
    senda, recva, recvq, kvb, zall, ka, kv, v0, v1, vg,
    sendo, attn, sendr, recvr, sendx, recvx, sendf, aud,
    in_sem,
    a_s, a_r, q_s, q_r, kv_s, kv_r, z_s, z_r, c_s, c_r, r_s, r_r, o_s, o_r, f_s, f_r,
):
    s = lax.axis_index("seq")
    y = lax.axis_index("head")
    z = s // (2 * NX)
    x = lax.rem(s // 2, NX)
    c = lax.rem(s, 2)
    other = 1 - c
    at = nz * 64
    vt = 2 * NX * 128

    def loop(lo, hi, body):
        def step(i, carry):
            body(i)
            return carry
        lax.fori_loop(lo, hi, step, 0)

    def at_x(d):
        return lax.rem(x + d, NX)

    def at_z(d):
        return lax.rem(z + d, nz)

    def at_y(d):
        return lax.rem(y + d, ny)

    def peer(zz, xx, cc, yy):
        return ((zz * NX + xx) * 2 + cc, yy)

    def remote(src, dst, ss, rs, to):
        return pltpu.make_async_remote_copy(
            src_ref=src, dst_ref=dst, send_sem=ss, recv_sem=rs, device_id=to, device_id_type=MESH
        )

    partner = peer(z, x, other, y)

    def arrived(dst, rs):
        remote(dst, dst, rs, rs, partner).wait_recv()

    def columns(ref, t):
        return ref.at[:, pl.ds(pl.multiple_of(t * 128, 128), 128)]

    local = [
        pltpu.make_async_copy(src, dst, in_sem.at[i])
        for i, (src, dst) in enumerate(
            [
                (aq, ina_q), (ak, ina_k), (av, ina_v),
                (columns(vq, x), recvq.at[x]),
                (columns(vk, x), kvb.at[c, x, 0]),
                (columns(vv, x), kvb.at[c, x, 1]),
                (wv_hbm, wv), (wa_hbm, wa),
            ]
        )
    ]
    for copy in local:
        copy.start()

    barrier = pltpu.get_barrier_semaphore()

    def greet(to):
        pl.semaphore_signal(barrier, inc=1, device_id=to, device_id_type=MESH)

    greet(partner)
    loop(1, nz, lambda d: greet(peer(at_z(d), x, c, y)))
    loop(1, NX * ny, lambda n: greet(peer(z, at_x(lax.rem(n, NX)), c, at_y(n // NX))))

    v_end = [vl[0]]
    a_end = [al[0]]
    for i in range(1, 4):
        v_end.append(v_end[-1] + vl[i])
        a_end.append(a_end[-1] + al[i])

    def clip_of(pos, ends):
        total = jnp.zeros_like(pos)
        for e in ends:
            total = total + (pos >= e).astype(jnp.int32)
        return total

    def iotas(shape):
        return [lax.broadcasted_iota(jnp.int32, shape, i) for i in range(len(shape))]

    def audio_pos(core, slab, row):
        pos = slab * 64 + (row >> 3) * 16 + core * 8 + (row & 7) + at // 2
        return jnp.where(pos >= at, pos - at, pos)

    place, row, lane = iotas((NX, 128, 128))
    token = ((z * NX + place) * 2 + c) * 128 + row
    tok_aug[...] = jnp.where(clip_of(token, v_end) == lane, 1.0, 0.0).astype(BF)
    core, slab, row, lane = iotas((2, nz, 32, 128))
    forbidden = (lane < 4) & (clip_of(audio_pos(core, slab, row), a_end) != lane)
    aud_aug[...] = jnp.where(forbidden, FORBID, 0.0).astype(BF)
    mark, col = iotas((128, NX * 128))
    for m in range(2):
        token = (z * NX + (col >> 7)) * 256 + m * 128 + (col & 127)
        kv[m, 128:256] = jnp.where(clip_of(token, v_end) == mark, 1.0, 0.0).astype(BF)
    mark, col = iotas((128, nz * 32))
    for m in range(2):
        forbidden = (mark < 4) & (clip_of(audio_pos(m, col >> 5, col & 31), a_end) != mark)
        marks = jnp.where(forbidden, FORBID, 0.0).astype(BF)
        ka[m, 128:256] = jnp.concatenate([marks, marks], axis=1)

    for i in range(3):
        local[i].wait()
    for p in range(NX):
        cols = pl.ds(128 * p, 128)
        k8, v8, q8 = (r[:, cols].astype(F32) for r in (ina_k, ina_v, ina_q))
        senda[p] = jnp.concatenate([k8, v8, q8, q8], axis=0).astype(BF)

    pl.semaphore_wait(barrier, 1 + nz - 1 + NX * ny - 1)

    def a_copy(d):
        t = at_x(d)
        return remote(senda.at[t], recva.at[x], a_s.at[t], a_r.at[x], peer(z, t, c, y))

    def q_copy(d):
        t = at_x(d)
        return remote(columns(vq, t), recvq.at[x], q_s.at[t], q_r.at[x], peer(z, t, c, y))

    def k_copy(d):
        t = at_x(d)
        return remote(columns(vk, t), kvb.at[c, x, 0], kv_s.at[0, t], kv_r.at[0, x], peer(z, t, c, y))

    def v_copy(d):
        t = at_x(d)
        return remote(columns(vv, t), kvb.at[c, x, 1], kv_s.at[1, t], kv_r.at[1, x], peer(z, t, c, y))

    for copy in (a_copy, k_copy, v_copy, q_copy):
        for d in range(1, NX):
            copy(d).start()

    recva[x] = senda[x]

    for d in range(1, NX):
        arrived(recva.at[at_x(d)], a_r.at[at_x(d)])
    got = recva[...].astype(F32)
    rows = [got[:, 8 * i : 8 * i + 8].reshape(32, 128) for i in range(3)]
    zall[c, z] = jnp.concatenate(rows, axis=0).astype(BF)

    def z_copy(d):
        t = at_z(d)
        return remote(zall.at[c, z], zall.at[c, z], z_s.at[t], z_r.at[z], peer(t, x, c, y))

    for d in range(1, nz):
        z_copy(d).start()

    z_share = remote(zall.at[c], zall.at[c], c_s.at[0], c_r.at[0], partner)
    kv_share = remote(kvb.at[c], kvb.at[c], c_s.at[1], c_r.at[1], partner)
    for i in (4, 5):
        local[i].wait()
    for n in range(1, NX):
        for i in range(2):
            arrived(kvb.at[c, at_x(n), i], kv_r.at[i, at_x(n)])
    kv_share.start()
    for d in range(1, nz):
        arrived(zall.at[c, at_z(d)], z_r.at[at_z(d)])
    z_share.start()

    low_row = low((1, 128))
    head0 = jnp.where(low_row, 1.0, 0.0).astype(BF)
    head1 = jnp.where(low_row, 0.0, 1.0).astype(BF)
    mine = jnp.where(c == 0, head0.astype(F32), head1.astype(F32)).astype(BF)
    rest = jnp.where(c == 0, head1.astype(F32), head0.astype(F32)).astype(BF)
    half_at = at // 2
    upper = lax.broadcasted_iota(jnp.int32, (128, half_at), 0) < 64

    def prepare_audio(m):
        rows = pl.ds(pl.multiple_of(m * half_at, half_at), half_at)
        key = zall[m, :, 0:32].reshape(half_at, 128).astype(F32).T
        ka[m, 0:128] = jnp.concatenate([jnp.where(upper, key, 0.0), jnp.where(upper, 0.0, key)], axis=1).astype(BF)
        value = zall[m, :, 32:64].reshape(half_at, 128)
        v0[rows] = value * head0 + head1
        v1[rows] = value * head1 + head0

    def prepare_video(m):
        rows = pl.ds(pl.multiple_of(m * (vt // 2), vt // 2), vt // 2)
        kv[m, 0:128] = kvb[m, :, 0].reshape(vt // 2, 128).astype(F32).T.astype(BF)
        vg[rows] = kvb[m, :, 1].reshape(vt // 2, 128) * mine + rest

    prepare_video(c)
    prepare_audio(c)
    local[3].wait()
    for d in range(1, NX):
        arrived(recvq.at[at_x(d)], q_r.at[at_x(d)])
    arrived(kvb.at[other], c_r.at[1])
    prepare_video(other)
    arrived(zall.at[other], c_r.at[0])
    prepare_audio(other)

    low128 = low((128, 128))

    def o_copy(t, e):
        u = at_y(e)
        return remote(sendo.at[t], attn.at[y, x], o_s.at[u, t], o_r.at[y, x], peer(z, t, c, u))

    def video_block(t):
        query = jnp.concatenate([recvq[t], tok_aug[t]], axis=1)
        scs = [nn_dot(query, ka[m]) for m in range(2)]
        outs = []
        for i, values in ((0, v0[...]), (1, v1[...])):
            half = jnp.concatenate([sc[:, i * half_at : (i + 1) * half_at] for sc in scs], axis=1)
            top = jnp.max(half, axis=1, keepdims=True)
            w = jnp.exp2((half - top) * SCALE).astype(BF)
            outs.append(nn_dot(w, values))
        num = jnp.where(low128, outs[0], outs[1])
        den = swap(jnp.where(low128, outs[1], outs[0]))
        return (num / den).astype(BF)

    def video_steps(ds):
        done = [video_block(at_x(d)) for d in ds]
        for d, block in zip(ds, done):
            sendo[at_x(d)] = block
        for d in ds:
            for e in range(ny) if d else range(1, ny):
                o_copy(at_x(d), e).start()

    lane128 = lanes((128, 128))

    def audio_block(p):
        query = zall[:, pl.ds(2 * p, 2), 64:96].reshape(128, 128) * mine
        query = jnp.concatenate([query, aud_aug[:, pl.ds(2 * p, 2)].reshape(128, 128)], axis=1)
        sc = jnp.concatenate([nn_dot(query, kv[m]) for m in range(2)], axis=1)
        top = jnp.max(sc, axis=1, keepdims=True)
        w = jnp.exp2((sc - top) * SCALE).astype(BF)
        full = nn_dot(w, vg[...])
        turned = swap(full)
        full, turned = jnp.where(c == 0, full, turned), jnp.where(c == 0, turned, full)
        mean = full / turned
        level = top * SCALE + jnp.log(jnp.where(low128, 1.0, full)) * LOG2E
        first = level.astype(BF).astype(F32)
        second = (level - first).astype(BF).astype(F32)
        third = level - first - second
        parts = jnp.where(lane128 < 96, first, jnp.where(lane128 < 112, second, third))
        out = jnp.where(low128, mean, parts).reshape(2, 2, 32, 128)
        return [out[:, i].reshape(64, 128).astype(BF) for i in range(2)]

    def r_copy(t):
        return remote(sendr.at[t], recvr.at[z], r_s.at[t], r_r.at[z], peer(t, x, c, y))

    def audio_steps(ds):
        ps = [lax.rem(z // 2 + d, nz // 2) for d in ds]
        done = [audio_block(p) for p in ps]
        for p, blocks in zip(ps, done):
            for i in range(2):
                sendr[2 * p + i] = blocks[i]
        for d, p in zip(ds, ps):
            if d:
                for i in range(2):
                    r_copy(2 * p + i).start()
            else:
                r_copy(2 * p + 1 - lax.rem(z, 2)).start()

    pairs = list(range(1, nz // 2)) + [0]
    for ds in VIDEO[0]:
        video_steps(ds)
    for i in range(0, len(pairs), AUDIO):
        audio_steps(pairs[i : i + AUDIO])
    recvr[z] = sendr[z]
    for ds in VIDEO[1]:
        video_steps(ds)
    attn[y, x] = sendo[x]

    loop(1, nz, lambda d: arrived(recvr.at[at_z(d)], r_r.at[at_z(d)]))
    part = recvr[...].astype(F32)
    level = part[:, :, 64:65] + part[:, :, 96:97] + part[:, :, 112:113]
    share = jnp.exp2(level - jnp.max(level, axis=0, keepdims=True))
    mixed = jnp.sum(part * share, axis=0) / jnp.sum(share, axis=0)
    mixed = jnp.where(c == 0, mixed, swap(mixed))
    sendx[...] = jnp.where(c == 0, mixed[32:64], mixed[0:32])
    x_share = remote(sendx, recvx, c_s.at[2], c_r.at[2], partner)
    x_share.start()
    arrived(recvx, c_r.at[2])
    mine32 = low((32, 128)) == (c == 0)
    both = jnp.where(mine32, jnp.where(c == 0, mixed[0:32], mixed[32:64]), recvx[...])
    sendf[...] = both.reshape(NX, 8, 128)

    def f_copy(n):
        t = at_x(lax.rem(n, NX))
        u = at_y(n // NX)
        return remote(sendf.at[t], aud.at[y, x], f_s.at[u, t], f_r.at[y, x], peer(z, t, c, u))

    loop(1, NX * ny, lambda n: f_copy(n).start())
    aud[y, x] = sendf[x]

    for copy in (a_copy, k_copy, v_copy, q_copy):
        for d in range(1, NX):
            copy(d).wait_send()
    for copy in (z_share, kv_share, x_share):
        copy.wait_send()

    def sent_ring(d):
        z_copy(d).wait_send()
        r_copy(at_z(d)).wait_send()

    loop(1, nz, sent_ring)
    loop(1, NX * ny, lambda n: o_copy(at_x(lax.rem(n, NX)), n // NX).wait_send())

    def wait_o(n):
        t = at_x(lax.rem(n, NX))
        u = at_y(n // NX)
        arrived(attn.at[u, t], o_r.at[u, t])

    loop(1, NX * ny, wait_o)
    every = [(u, t) for u in range(ny) for t in range(NX)]
    local[6].wait()
    hidden = jnp.concatenate([attn[u, t] for u, t in every], axis=1)
    width = wv.shape[1] // 4
    for n in range(4):
        cols = pl.ds(n * width, width)
        vo[:, cols] = nn_dot(hidden, wv[:, cols]).astype(BF)

    def wait_f(n):
        t = at_x(lax.rem(n, NX))
        u = at_y(n // NX)
        arrived(aud.at[u, t], f_r.at[u, t])

    loop(1, NX * ny, wait_f)
    local[7].wait()
    hidden = jnp.concatenate([aud[u, t] for u, t in every], axis=1).astype(BF)
    ao[...] = nn_dot(hidden, wa[...]).astype(BF)

    loop(1, NX * ny, lambda n: f_copy(n).wait_send())


def write_out(v_in, a_in, v_out, a_out, sem):
    copies = [pltpu.make_async_copy(v_in, v_out, sem.at[0]), pltpu.make_async_copy(a_in, a_out, sem.at[1])]
    for copy in copies:
        copy.start()
    for copy in copies:
        copy.wait()


def per_device(nz, ny, vq, vk, vv, aq, ak, av, vl, al, wv, wa):
    rows, width = vq.shape
    a_rows = aq.shape[0]
    at = nz * 64
    vt = 2 * NX * 128
    hbm = pl.BlockSpec(memory_space=pl.ANY)
    smem = pl.BlockSpec(memory_space=pltpu.SMEM)
    vmem = pl.BlockSpec(memory_space=pltpu.VMEM)
    bf = lambda *shape: pltpu.VMEM(shape, BF)
    wide = lambda *shape: pltpu.VMEM(shape, F32)
    dma = lambda *shape: pltpu.SemaphoreType.DMA(shape)

    def body(*refs):
        kernel(nz, ny, *refs)

    made = pl.pallas_call(
        body,
        out_shape=(
            pltpu.VMEM((rows, wv.shape[1]), BF),
            pltpu.VMEM((a_rows, wa.shape[1]), BF),
        ),
        in_specs=[smem, smem] + [hbm] * 8,
        out_specs=(vmem, vmem),
        scratch_shapes=[
            bf(a_rows, width), bf(a_rows, width), bf(a_rows, width),
            bf(*wv.shape), bf(*wa.shape),
            bf(NX, 128, 128), bf(2, nz, 32, 128),
            bf(NX, 32, 128), bf(NX, 32, 128), bf(NX, 128, 128), bf(2, NX, 2, 128, 128),
            bf(2, nz, 96, 128),
            bf(2, 256, at), bf(2, 256, vt // 2), bf(at, 128), bf(at, 128), bf(vt, 128),
            bf(NX, 128, 128), bf(ny, NX, 128, 128),
            bf(nz, 64, 128), bf(nz, 64, 128),
            wide(32, 128), wide(32, 128), wide(NX, 8, 128), wide(ny, NX, 8, 128),
            dma(8),
            dma(NX), dma(NX), dma(NX), dma(NX), dma(2, NX), dma(2, NX),
            dma(nz), dma(nz), dma(3), dma(3), dma(nz), dma(nz),
            dma(ny, NX), dma(ny, NX), dma(ny, NX), dma(ny, NX),
        ],
        compiler_params=pltpu.CompilerParams(
            collective_id=0, has_side_effects=True, vmem_limit_bytes=56 * 1024 * 1024
        ),
        name="cross_attention",
    )(vl, al, vq, vk, vv, aq, ak, av, wv, wa)
    shapes = (jax.ShapeDtypeStruct((rows, wv.shape[1]), BF), jax.ShapeDtypeStruct((a_rows, wa.shape[1]), BF))
    return pl.pallas_call(
        write_out,
        out_shape=shapes,
        in_specs=[vmem, vmem],
        out_specs=(hbm, hbm),
        scratch_shapes=[dma(2)],
        name="write_out",
    )(*(pltpu.with_memory_space_constraint(m, pltpu.VMEM) for m in made))


def solution(mesh):
    nz = mesh.shape["seq"] // (2 * NX)
    ny = mesh.shape["head"]

    def program(*arrays):
        return per_device(nz, ny, *arrays)

    return jax.shard_map(
        program,
        mesh=mesh,
        in_specs=(*(P("seq", "head"),) * 6, P(), P(), P(None, "head"), P(None, "head")),
        out_specs=(P("seq", "head"), P("seq", "head")),
        check_vma=False,
    )
```

```python
import math

import jax
import jax.numpy as jnp
from jax import lax
from jax.experimental import pallas as pl
from jax.experimental.pallas import tpu as pltpu
from jax.sharding import PartitionSpec as P

HEAD_DIM = 64
NX = 4
VIDEO = [[[1, 2]], [[3, 0]]]
AUDIO = 2
MESH = pl.DeviceIdType.MESH
BF = jnp.bfloat16
F32 = jnp.float32
FORBID = -65536.0
LOG2E = math.log2(math.e)
SCALE = LOG2E / math.sqrt(HEAD_DIM)


def nn_dot(a, b):
    return lax.dot_general(a, b, (((1,), (0,)), ((), ())), preferred_element_type=F32)


def swap(x):
    return pltpu.roll(x, 64, x.ndim - 1)


def lanes(shape):
    return lax.broadcasted_iota(jnp.int32, shape, len(shape) - 1)


def low(shape):
    return lanes(shape) < 64


def kernel(
    nz, ny,
    vl, al, vq, vk, vv, aq, ak, av, wv_hbm, wa_hbm,
    vo, ao,
    ina_q, ina_k, ina_v, wv, wa,
    tok_aug, aud_aug,
    senda, recva, recvq, kvb, zall, ka, kv, v0, v1, vg,
    sendo, attn, sendr, recvr, sendf, aud,
    in_sem,
    a_s, a_r, q_s, q_r, kv_s, kv_r, z_s, z_r, c_s, c_r, r_s, r_r, o_s, o_r, f_s, f_r,
):
    s = lax.axis_index("seq")
    y = lax.axis_index("head")
    z = s // (2 * NX)
    x = lax.rem(s // 2, NX)
    c = lax.rem(s, 2)
    other = 1 - c
    at = nz * 64
    vt = 2 * NX * 128

    def loop(lo, hi, body):
        for i in range(lo, hi):
            body(i)

    def at_x(d):
        return lax.rem(x + d, NX)

    def at_z(d):
        return lax.rem(z + d, nz)

    def at_y(d):
        return lax.rem(y + d, ny)

    def peer(zz, xx, cc, yy):
        return ((zz * NX + xx) * 2 + cc, yy)

    def remote(src, dst, ss, rs, to):
        return pltpu.make_async_remote_copy(
            src_ref=src, dst_ref=dst, send_sem=ss, recv_sem=rs, device_id=to, device_id_type=MESH
        )

    partner = peer(z, x, other, y)

    def arrived(dst, rs):
        remote(dst, dst, rs, rs, partner).wait_recv()

    def columns(ref, t):
        return ref.at[:, pl.ds(pl.multiple_of(t * 128, 128), 128)]

    local = [
        pltpu.make_async_copy(src, dst, in_sem.at[i])
        for i, (src, dst) in enumerate(
            [
                (aq, ina_q), (ak, ina_k), (av, ina_v),
                (columns(vq, x), recvq.at[x]),
                (columns(vk, x), kvb.at[c, x, 0]),
                (columns(vv, x), kvb.at[c, x, 1]),
                (wv_hbm, wv), (wa_hbm, wa),
            ]
        )
    ]
    for copy in local[:6]:
        copy.start()

    barrier = pltpu.get_barrier_semaphore()

    def greet(to):
        pl.semaphore_signal(barrier, inc=1, device_id=to, device_id_type=MESH)

    for d in range(1, NX):
        greet(peer(z, at_x(d), c, y))
    for d in sorted(range(1, nz), key=lambda d: abs(d - nz // 2)):
        greet(peer(at_z(d), x, c, y))
    greet(partner)
    for d in range(1, ny):
        greet(peer(z, x, c, at_y(d)))

    v_end = [vl[0]]
    a_end = [al[0]]
    for i in range(1, 4):
        v_end.append(v_end[-1] + vl[i])
        a_end.append(a_end[-1] + al[i])

    def clip_of(pos, ends):
        total = jnp.zeros_like(pos)
        for e in ends:
            total = total + (pos >= e).astype(jnp.int32)
        return total

    def iotas(shape):
        return [lax.broadcasted_iota(jnp.int32, shape, i) for i in range(len(shape))]

    def audio_pos(core, slab, row):
        pos = slab * 64 + (row >> 3) * 16 + core * 8 + (row & 7) + at // 2
        return jnp.where(pos >= at, pos - at, pos)

    place, row, lane = iotas((NX, 128, 128))
    token = ((z * NX + place) * 2 + c) * 128 + row
    tok_aug[...] = jnp.where(clip_of(token, v_end) == lane, 1.0, 0.0).astype(BF)
    core, slab, row, lane = iotas((2, nz, 32, 128))
    forbidden = (lane < 4) & (clip_of(audio_pos(core, slab, row), a_end) != lane)
    aud_aug[...] = jnp.where(forbidden, FORBID, 0.0).astype(BF)
    mark, col = iotas((128, NX * 128))
    for m in range(2):
        token = (z * NX + (col >> 7)) * 256 + m * 128 + (col & 127)
        kv[m, 128:256] = jnp.where(clip_of(token, v_end) == mark, 1.0, 0.0).astype(BF)
    mark, col = iotas((128, nz * 32))
    for m in range(2):
        forbidden = (mark < 4) & (clip_of(audio_pos(m, col >> 5, col & 31), a_end) != mark)
        marks = jnp.where(forbidden, FORBID, 0.0).astype(BF)
        ka[m, 128:256] = jnp.concatenate([marks, marks], axis=1)

    for i in range(3):
        local[i].wait()
    for p in range(NX):
        cols = pl.ds(128 * p, 128)
        k8, v8, q8 = (r[:, cols].astype(F32) for r in (ina_k, ina_v, ina_q))
        senda[p] = jnp.concatenate([k8, v8, q8, q8], axis=0).astype(BF)

    pl.semaphore_wait(barrier, 1 + nz - 1 + NX - 1 + ny - 1)

    def a_copy(d):
        t = at_x(d)
        return remote(senda.at[t], recva.at[x], a_s.at[t], a_r.at[x], peer(z, t, c, y))

    def q_copy(d):
        t = at_x(d)
        return remote(columns(vq, t), recvq.at[x], q_s.at[t], q_r.at[x], peer(z, t, c, y))

    def k_copy(d):
        t = at_x(d)
        return remote(columns(vk, t), kvb.at[c, x, 0], kv_s.at[0, t], kv_r.at[0, x], peer(z, t, c, y))

    def v_copy(d):
        t = at_x(d)
        return remote(columns(vv, t), kvb.at[c, x, 1], kv_s.at[1, t], kv_r.at[1, x], peer(z, t, c, y))

    for copy in (a_copy, k_copy, v_copy, q_copy):
        for d in range(1, NX):
            copy(d).start()

    for copy in local[6:]:
        copy.start()
    recva[x] = senda[x]

    for d in range(1, NX):
        arrived(recva.at[at_x(d)], a_r.at[at_x(d)])
    got = recva[...].astype(F32)
    rows = [got[:, 8 * i : 8 * i + 8].reshape(32, 128) for i in range(3)]
    zall[c, z] = jnp.concatenate(rows, axis=0).astype(BF)

    def z_copy(d):
        t = at_z(d)
        return remote(zall.at[c, z], zall.at[c, z], z_s.at[t], z_r.at[z], peer(t, x, c, y))

    for d in sorted(range(1, nz), key=lambda d: abs(d - nz // 2)):
        z_copy(d).start()

    z_share = remote(zall.at[c], zall.at[c], c_s.at[0], c_r.at[0], partner)
    kv_share = remote(kvb.at[c], kvb.at[c], c_s.at[1], c_r.at[1], partner)
    for i in (4, 5):
        local[i].wait()
    for n in range(1, NX):
        for i in range(2):
            arrived(kvb.at[c, at_x(n), i], kv_r.at[i, at_x(n)])
    kv_share.start()
    for d in range(1, nz):
        arrived(zall.at[c, at_z(d)], z_r.at[at_z(d)])
    z_share.start()

    low_row = low((1, 128))
    head0 = jnp.where(low_row, 1.0, 0.0).astype(BF)
    head1 = jnp.where(low_row, 0.0, 1.0).astype(BF)
    mine = jnp.where(c == 0, head0.astype(F32), head1.astype(F32)).astype(BF)
    rest = jnp.where(c == 0, head1.astype(F32), head0.astype(F32)).astype(BF)
    half_at = at // 2
    upper = lax.broadcasted_iota(jnp.int32, (128, half_at), 0) < 64

    def prepare_audio(m):
        rows = pl.ds(pl.multiple_of(m * half_at, half_at), half_at)
        key = zall[m, :, 0:32].reshape(half_at, 128).astype(F32).T
        ka[m, 0:128] = jnp.concatenate([jnp.where(upper, key, 0.0), jnp.where(upper, 0.0, key)], axis=1).astype(BF)
        value = zall[m, :, 32:64].reshape(half_at, 128)
        v0[rows] = value * head0 + head1
        v1[rows] = value * head1 + head0

    def prepare_video(m):
        rows = pl.ds(pl.multiple_of(m * (vt // 2), vt // 2), vt // 2)
        kv[m, 0:128] = kvb[m, :, 0].reshape(vt // 2, 128).astype(F32).T.astype(BF)
        vg[rows] = kvb[m, :, 1].reshape(vt // 2, 128) * mine + rest

    prepare_video(c)
    prepare_audio(c)
    local[3].wait()
    for d in range(1, NX):
        arrived(recvq.at[at_x(d)], q_r.at[at_x(d)])
    arrived(kvb.at[other], c_r.at[1])
    prepare_video(other)
    arrived(zall.at[other], c_r.at[0])
    prepare_audio(other)

    low128 = low((128, 128))

    def o_copy(t, e):
        u = at_y(e)
        return remote(sendo.at[t], attn.at[y, x], o_s.at[u, t], o_r.at[y, x], peer(z, t, c, u))

    def video_block(t):
        query = jnp.concatenate([recvq[t], tok_aug[t]], axis=1)
        scs = [nn_dot(query, ka[m]) for m in range(2)]
        outs = []
        for i, values in ((0, v0[...]), (1, v1[...])):
            half = jnp.concatenate([sc[:, i * half_at : (i + 1) * half_at] for sc in scs], axis=1)
            top = jnp.max(half, axis=1, keepdims=True)
            w = jnp.exp2((half - top) * SCALE).astype(BF)
            outs.append(nn_dot(w, values))
        num = jnp.where(low128, outs[0], outs[1])
        den = swap(jnp.where(low128, outs[1], outs[0]))
        return (num / den).astype(BF)

    def video_steps(ds):
        done = [video_block(at_x(d)) for d in ds]
        for d, block in zip(ds, done):
            sendo[at_x(d)] = block
        for d in ds:
            for e in range(ny) if d else range(1, ny):
                o_copy(at_x(d), e).start()

    lane128 = lanes((128, 128))

    def audio_block(p):
        query = zall[:, pl.ds(2 * p, 2), 64:96].reshape(128, 128) * mine
        query = jnp.concatenate([query, aud_aug[:, pl.ds(2 * p, 2)].reshape(128, 128)], axis=1)
        sc = jnp.concatenate([nn_dot(query, kv[m]) for m in range(2)], axis=1)
        top = jnp.max(sc, axis=1, keepdims=True)
        w = jnp.exp2((sc - top) * SCALE).astype(BF)
        full = nn_dot(w, vg[...])
        turned = swap(full)
        full, turned = jnp.where(c == 0, full, turned), jnp.where(c == 0, turned, full)
        mean = full / turned
        level = top * SCALE + jnp.log(jnp.where(low128, 1.0, full)) * LOG2E
        first = level.astype(BF).astype(F32)
        second = (level - first).astype(BF).astype(F32)
        third = level - first - second
        parts = jnp.where(lane128 < 96, first, jnp.where(lane128 < 112, second, third))
        return jnp.where(low128, mean, parts).reshape(2, 2, 32, 128).astype(BF)

    def r_copy(t, m):
        return remote(sendr.at[m, t], recvr.at[c, z], r_s.at[m, t], r_r.at[c, z], peer(t, x, m, y))

    def audio_steps(ds):
        ps = [lax.rem(z // 2 + d, nz // 2) for d in ds]
        done = [audio_block(p) for p in ps]
        for p, blocks in zip(ps, done):
            sendr[:, pl.ds(2 * p, 2)] = blocks
        for d, p in zip(ds, ps):
            for m in range(2):
                if d:
                    for i in range(2):
                        r_copy(2 * p + i, m).start()
                else:
                    r_copy(2 * p + 1 - lax.rem(z, 2), m).start()
            if d == 0:
                r_copy(z, other).start()

    pairs = list(range(1, nz // 2)) + [0]
    for ds in VIDEO[0]:
        video_steps(ds)
    for i in range(0, len(pairs), AUDIO):
        audio_steps(pairs[i : i + AUDIO])
    recvr[c, z] = sendr[c, z]
    for ds in VIDEO[1]:
        video_steps(ds)
    attn[y, x] = sendo[x]

    arrived(recvr.at[other, z], r_r.at[other, z])
    for d in range(1, nz):
        for m in range(2):
            arrived(recvr.at[m, at_z(d)], r_r.at[m, at_z(d)])
    part = recvr[...].astype(F32)
    level = part[:, :, :, 64:65] + part[:, :, :, 96:97] + part[:, :, :, 112:113]
    share = jnp.exp2(level - jnp.max(level, axis=1, keepdims=True))
    mixed = jnp.sum(part * share, axis=1) / jnp.sum(share, axis=1)
    both = jnp.where(low((32, 128)), mixed[0], swap(mixed[1]))
    sendf[...] = both.reshape(NX, 8, 128)

    def f_copy(n):
        t = at_x(n % NX)
        u = at_y(n // NX)
        return remote(sendf.at[t], aud.at[y, x], f_s.at[u, t], f_r.at[y, x], peer(z, t, c, u))

    loop(1, NX * ny, lambda n: f_copy(n).start())
    aud[y, x] = sendf[x]

    for copy in (a_copy, k_copy, v_copy, q_copy):
        for d in range(1, NX):
            copy(d).wait_send()
    for copy in (z_share, kv_share):
        copy.wait_send()

    def sent_ring(d):
        z_copy(d).wait_send()
        for m in range(2):
            r_copy(at_z(d), m).wait_send()

    loop(1, nz, sent_ring)
    r_copy(z, other).wait_send()
    loop(1, NX * ny, lambda n: o_copy(at_x(n % NX), n // NX).wait_send())

    def wait_o(n):
        t = at_x(n % NX)
        u = at_y(n // NX)
        arrived(attn.at[u, t], o_r.at[u, t])

    loop(1, NX * ny, wait_o)
    every = [(u, t) for u in range(ny) for t in range(NX)]
    local[6].wait()
    hidden = jnp.concatenate([attn[u, t] for u, t in every], axis=1)
    width = wv.shape[1] // 4
    for n in range(4):
        cols = pl.ds(n * width, width)
        vo[:, cols] = nn_dot(hidden, wv[:, cols]).astype(BF)

    def wait_f(n):
        t = at_x(n % NX)
        u = at_y(n // NX)
        arrived(aud.at[u, t], f_r.at[u, t])

    loop(1, NX * ny, wait_f)
    local[7].wait()
    hidden = jnp.concatenate([aud[u, t] for u, t in every], axis=1).astype(BF)
    ao[...] = nn_dot(hidden, wa[...]).astype(BF)

    loop(1, NX * ny, lambda n: f_copy(n).wait_send())


def write_out(v_in, a_in, v_out, a_out, sem):
    copies = [pltpu.make_async_copy(v_in, v_out, sem.at[0]), pltpu.make_async_copy(a_in, a_out, sem.at[1])]
    for copy in copies:
        copy.start()
    for copy in copies:
        copy.wait()


def per_device(nz, ny, vq, vk, vv, aq, ak, av, vl, al, wv, wa):
    rows, width = vq.shape
    a_rows = aq.shape[0]
    at = nz * 64
    vt = 2 * NX * 128
    hbm = pl.BlockSpec(memory_space=pl.ANY)
    smem = pl.BlockSpec(memory_space=pltpu.SMEM)
    vmem = pl.BlockSpec(memory_space=pltpu.VMEM)
    bf = lambda *shape: pltpu.VMEM(shape, BF)
    wide = lambda *shape: pltpu.VMEM(shape, F32)
    dma = lambda *shape: pltpu.SemaphoreType.DMA(shape)

    def body(*refs):
        kernel(nz, ny, *refs)

    made = pl.pallas_call(
        body,
        out_shape=(
            pltpu.VMEM((rows, wv.shape[1]), BF),
            pltpu.VMEM((a_rows, wa.shape[1]), BF),
        ),
        in_specs=[smem, smem] + [hbm] * 8,
        out_specs=(vmem, vmem),
        scratch_shapes=[
            bf(a_rows, width), bf(a_rows, width), bf(a_rows, width),
            bf(*wv.shape), bf(*wa.shape),
            bf(NX, 128, 128), bf(2, nz, 32, 128),
            bf(NX, 32, 128), bf(NX, 32, 128), bf(NX, 128, 128), bf(2, NX, 2, 128, 128),
            bf(2, nz, 96, 128),
            bf(2, 256, at), bf(2, 256, vt // 2), bf(at, 128), bf(at, 128), bf(vt, 128),
            bf(NX, 128, 128), bf(ny, NX, 128, 128),
            bf(2, nz, 32, 128), bf(2, nz, 32, 128),
            wide(NX, 8, 128), wide(ny, NX, 8, 128),
            dma(8),
            dma(NX), dma(NX), dma(NX), dma(NX), dma(2, NX), dma(2, NX),
            dma(nz), dma(nz), dma(2), dma(2), dma(2, nz), dma(2, nz),
            dma(ny, NX), dma(ny, NX), dma(ny, NX), dma(ny, NX),
        ],
        compiler_params=pltpu.CompilerParams(
            collective_id=0, has_side_effects=True, vmem_limit_bytes=56 * 1024 * 1024
        ),
        name="cross_attention",
    )(vl, al, vq, vk, vv, aq, ak, av, wv, wa)
    shapes = (jax.ShapeDtypeStruct((rows, wv.shape[1]), BF), jax.ShapeDtypeStruct((a_rows, wa.shape[1]), BF))
    return pl.pallas_call(
        write_out,
        out_shape=shapes,
        in_specs=[vmem, vmem],
        out_specs=(hbm, hbm),
        scratch_shapes=[dma(2)],
        name="write_out",
    )(*(pltpu.with_memory_space_constraint(m, pltpu.VMEM) for m in made))


def solution(mesh):
    nz = mesh.shape["seq"] // (2 * NX)
    ny = mesh.shape["head"]

    def program(*arrays):
        return per_device(nz, ny, *arrays)

    return jax.shard_map(
        program,
        mesh=mesh,
        in_specs=(*(P("seq", "head"),) * 6, P(), P(), P(None, "head"), P(None, "head")),
        out_specs=(P("seq", "head"), P("seq", "head")),
        check_vma=False,
    )
```

```python
import math

import jax
import jax.numpy as jnp
from jax import lax
from jax.experimental import pallas as pl
from jax.experimental.pallas import tpu as pltpu
from jax.sharding import PartitionSpec as P

HEAD_DIM = 64
NX = 4
VIDEO = [[[1, 2]], [[3, 0]]]
AUDIO = 2
MESH = pl.DeviceIdType.MESH
BF = jnp.bfloat16
F32 = jnp.float32
FORBID = -65536.0
LOG2E = math.log2(math.e)
SCALE = LOG2E / math.sqrt(HEAD_DIM)


def nn_dot(a, b):
    return lax.dot_general(a, b, (((1,), (0,)), ((), ())), preferred_element_type=F32)


def swap(x):
    return pltpu.roll(x, 64, x.ndim - 1)


def lanes(shape):
    return lax.broadcasted_iota(jnp.int32, shape, len(shape) - 1)


def low(shape):
    return lanes(shape) < 64


def kernel(
    nz, ny,
    vl, al, vq, vk, vv, aq, ak, av, wv_hbm, wa_hbm,
    vo, ao,
    ina_q, ina_k, ina_v, wv, wa,
    tok_aug, aud_aug,
    senda, recva, recvq, kvb, zall, ka, kv, v0, v1, vg,
    sendo, attn, sendr, recvr, sendf, aud,
    in_sem,
    a_s, a_r, q_s, q_r, kv_s, kv_r, z_s, z_r, c_s, c_r, r_s, r_r, o_s, o_r, f_s, f_r,
):
    s = lax.axis_index("seq")
    y = lax.axis_index("head")
    z = s // (2 * NX)
    x = lax.rem(s // 2, NX)
    c = lax.rem(s, 2)
    other = 1 - c
    at = nz * 64
    vt = 2 * NX * 128

    def loop(lo, hi, body):
        for i in range(lo, hi):
            body(i)

    def at_x(d):
        return lax.rem(x + d, NX)

    def at_z(d):
        return lax.rem(z + d, nz)

    def at_y(d):
        return lax.rem(y + d, ny)

    def peer(zz, xx, cc, yy):
        return ((zz * NX + xx) * 2 + cc, yy)

    def remote(src, dst, ss, rs, to):
        return pltpu.make_async_remote_copy(
            src_ref=src, dst_ref=dst, send_sem=ss, recv_sem=rs, device_id=to, device_id_type=MESH
        )

    partner = peer(z, x, other, y)

    def arrived(dst, rs):
        remote(dst, dst, rs, rs, partner).wait_recv()

    def columns(ref, t):
        return ref.at[:, pl.ds(pl.multiple_of(t * 128, 128), 128)]

    local = [
        pltpu.make_async_copy(src, dst, in_sem.at[i])
        for i, (src, dst) in enumerate(
            [
                (aq, ina_q), (ak, ina_k), (av, ina_v),
                (columns(vq, x), recvq.at[x]),
                (columns(vk, x), kvb.at[c, x, 0]),
                (columns(vv, x), kvb.at[c, x, 1]),
                (wv_hbm, wv), (wa_hbm, wa),
            ]
        )
    ]
    for copy in local[:6]:
        copy.start()

    barrier = pltpu.get_barrier_semaphore()

    def greet(to):
        pl.semaphore_signal(barrier, inc=1, device_id=to, device_id_type=MESH)

    for d in range(1, NX):
        greet(peer(z, at_x(d), c, y))
    for d in sorted(range(1, nz), key=lambda d: abs(d - nz // 2)):
        greet(peer(at_z(d), x, c, y))
    greet(partner)
    for d in range(1, ny):
        greet(peer(z, x, c, at_y(d)))

    v_end = [vl[0]]
    a_end = [al[0]]
    for i in range(1, 4):
        v_end.append(v_end[-1] + vl[i])
        a_end.append(a_end[-1] + al[i])

    def clip_of(pos, ends):
        total = jnp.zeros_like(pos)
        for e in ends:
            total = total + (pos >= e).astype(jnp.int32)
        return total

    def iotas(shape):
        return [lax.broadcasted_iota(jnp.int32, shape, i) for i in range(len(shape))]

    def audio_pos(core, slab, row):
        pos = slab * 64 + (row >> 3) * 16 + core * 8 + (row & 7) + at // 2
        return jnp.where(pos >= at, pos - at, pos)

    place, row, lane = iotas((NX, 128, 128))
    token = ((z * NX + place) * 2 + c) * 128 + row
    tok_aug[...] = jnp.where(clip_of(token, v_end) == lane, 1.0, 0.0).astype(BF)
    core, slab, row, lane = iotas((2, nz, 32, 128))
    forbidden = (lane < 4) & (clip_of(audio_pos(core, slab, row), a_end) != lane)
    aud_aug[...] = jnp.where(forbidden, FORBID, 0.0).astype(BF)
    mark, col = iotas((128, NX * 128))
    for m in range(2):
        token = (z * NX + (col >> 7)) * 256 + m * 128 + (col & 127)
        kv[m, 128:256] = jnp.where(clip_of(token, v_end) == mark, 1.0, 0.0).astype(BF)
    mark, col = iotas((128, nz * 32))
    for m in range(2):
        forbidden = (mark < 4) & (clip_of(audio_pos(m, col >> 5, col & 31), a_end) != mark)
        marks = jnp.where(forbidden, FORBID, 0.0).astype(BF)
        ka[m, 128:256] = jnp.concatenate([marks, marks], axis=1)

    for i in range(3):
        local[i].wait()
    for p in range(NX):
        cols = pl.ds(128 * p, 128)
        k8, v8, q8 = (r[:, cols].astype(F32) for r in (ina_k, ina_v, ina_q))
        senda[p] = jnp.concatenate([k8, v8, q8, q8], axis=0).astype(BF)

    pl.semaphore_wait(barrier, 1 + nz - 1 + NX - 1 + ny - 1)

    def a_copy(d):
        t = at_x(d)
        return remote(senda.at[t], recva.at[x], a_s.at[t], a_r.at[x], peer(z, t, c, y))

    def q_copy(d):
        t = at_x(d)
        return remote(columns(vq, t), recvq.at[x], q_s.at[t], q_r.at[x], peer(z, t, c, y))

    def k_copy(d):
        t = at_x(d)
        return remote(columns(vk, t), kvb.at[c, x, 0], kv_s.at[0, t], kv_r.at[0, x], peer(z, t, c, y))

    def v_copy(d):
        t = at_x(d)
        return remote(columns(vv, t), kvb.at[c, x, 1], kv_s.at[1, t], kv_r.at[1, x], peer(z, t, c, y))

    for copy in (a_copy, k_copy, v_copy, q_copy):
        for d in range(1, NX):
            copy(d).start()

    for copy in local[6:]:
        copy.start()
    recva[x] = senda[x]

    for d in range(1, NX):
        arrived(recva.at[at_x(d)], a_r.at[at_x(d)])
    got = recva[...].astype(F32)
    rows = [got[:, 8 * i : 8 * i + 8].reshape(32, 128) for i in range(3)]
    zall[c, z] = jnp.concatenate(rows, axis=0).astype(BF)

    def z_copy(d):
        t = at_z(d)
        return remote(zall.at[c, z], zall.at[c, z], z_s.at[t], z_r.at[z], peer(t, x, c, y))

    for d in sorted(range(1, nz), key=lambda d: abs(d - nz // 2)):
        z_copy(d).start()

    z_share = remote(zall.at[c], zall.at[c], c_s.at[0], c_r.at[0], partner)
    kv_share = remote(kvb.at[c], kvb.at[c], c_s.at[1], c_r.at[1], partner)
    for i in (4, 5):
        local[i].wait()
    for n in range(1, NX):
        for i in range(2):
            arrived(kvb.at[c, at_x(n), i], kv_r.at[i, at_x(n)])
    kv_share.start()
    low_row = low((1, 128))
    head0 = jnp.where(low_row, 1.0, 0.0).astype(BF)
    head1 = jnp.where(low_row, 0.0, 1.0).astype(BF)
    mine = jnp.where(c == 0, head0.astype(F32), head1.astype(F32)).astype(BF)
    rest = jnp.where(c == 0, head1.astype(F32), head0.astype(F32)).astype(BF)
    half_at = at // 2
    upper = lax.broadcasted_iota(jnp.int32, (128, half_at), 0) < 64

    def prepare_audio(m):
        rows = pl.ds(pl.multiple_of(m * half_at, half_at), half_at)
        key = zall[m, :, 0:32].reshape(half_at, 128).astype(F32).T
        ka[m, 0:128] = jnp.concatenate([jnp.where(upper, key, 0.0), jnp.where(upper, 0.0, key)], axis=1).astype(BF)
        value = zall[m, :, 32:64].reshape(half_at, 128)
        v0[rows] = value * head0 + head1
        v1[rows] = value * head1 + head0

    def prepare_video(m):
        rows = pl.ds(pl.multiple_of(m * (vt // 2), vt // 2), vt // 2)
        kv[m, 0:128] = kvb[m, :, 0].reshape(vt // 2, 128).astype(F32).T.astype(BF)
        vg[rows] = kvb[m, :, 1].reshape(vt // 2, 128) * mine + rest

    prepare_video(c)
    for d in range(1, nz):
        arrived(zall.at[c, at_z(d)], z_r.at[at_z(d)])
    z_share.start()

    prepare_audio(c)
    local[3].wait()
    for d in range(1, NX):
        arrived(recvq.at[at_x(d)], q_r.at[at_x(d)])
    arrived(zall.at[other], c_r.at[0])
    prepare_audio(other)

    low128 = low((128, 128))

    def o_copy(t, e):
        u = at_y(e)
        return remote(sendo.at[t], attn.at[y, x], o_s.at[u, t], o_r.at[y, x], peer(z, t, c, u))

    def video_block(t):
        query = jnp.concatenate([recvq[t], tok_aug[t]], axis=1)
        scs = [nn_dot(query, ka[m]) for m in range(2)]
        outs = []
        for i, values in ((0, v0[...]), (1, v1[...])):
            half = jnp.concatenate([sc[:, i * half_at : (i + 1) * half_at] for sc in scs], axis=1)
            top = jnp.max(half, axis=1, keepdims=True)
            w = jnp.exp2((half - top) * SCALE).astype(BF)
            outs.append(nn_dot(w, values))
        num = jnp.where(low128, outs[0], outs[1])
        den = swap(jnp.where(low128, outs[1], outs[0]))
        return (num / den).astype(BF)

    def video_steps(ds):
        done = [video_block(at_x(d)) for d in ds]
        for d, block in zip(ds, done):
            sendo[at_x(d)] = block
        for d in ds:
            for e in sorted(range(0 if d else 1, ny), key=lambda e: abs(e - ny // 2)):
                o_copy(at_x(d), e).start()

    lane128 = lanes((128, 128))

    def audio_block(p):
        query = zall[:, pl.ds(2 * p, 2), 64:96].reshape(128, 128) * mine
        query = jnp.concatenate([query, aud_aug[:, pl.ds(2 * p, 2)].reshape(128, 128)], axis=1)
        sc = jnp.concatenate([nn_dot(query, kv[m]) for m in range(2)], axis=1)
        top = jnp.max(sc, axis=1, keepdims=True)
        w = jnp.exp2((sc - top) * SCALE).astype(BF)
        full = nn_dot(w, vg[...])
        turned = swap(full)
        full, turned = jnp.where(c == 0, full, turned), jnp.where(c == 0, turned, full)
        mean = full / turned
        level = top * SCALE + jnp.log(jnp.where(low128, 1.0, full)) * LOG2E
        first = level.astype(BF).astype(F32)
        second = (level - first).astype(BF).astype(F32)
        third = level - first - second
        parts = jnp.where(lane128 < 96, first, jnp.where(lane128 < 112, second, third))
        return jnp.where(low128, mean, parts).reshape(2, 2, 32, 128).astype(BF)

    def r_copy(t, m):
        return remote(sendr.at[m, t], recvr.at[c, z], r_s.at[m, t], r_r.at[c, z], peer(t, x, m, y))

    def audio_steps(ds):
        ps = [lax.rem(z // 2 + d, nz // 2) for d in ds]
        done = [audio_block(p) for p in ps]
        for p, blocks in zip(ps, done):
            sendr[:, pl.ds(2 * p, 2)] = blocks
        for d, p in zip(ds, ps):
            for m in range(2):
                if d:
                    for i in range(2):
                        r_copy(2 * p + i, m).start()
                else:
                    r_copy(2 * p + 1 - lax.rem(z, 2), m).start()
            if d == 0:
                r_copy(z, other).start()

    pairs = sorted(range(1, nz // 2), key=lambda d: abs(d - nz // 4)) + [0]
    for ds in VIDEO[0]:
        video_steps(ds)
    arrived(kvb.at[other], c_r.at[1])
    prepare_video(other)
    for i in range(0, len(pairs), AUDIO):
        audio_steps(pairs[i : i + AUDIO])
    recvr[c, z] = sendr[c, z]
    for ds in VIDEO[1]:
        video_steps(ds)
    attn[y, x] = sendo[x]

    arrived(recvr.at[other, z], r_r.at[other, z])
    for d in range(1, nz):
        for m in range(2):
            arrived(recvr.at[m, at_z(d)], r_r.at[m, at_z(d)])
    part = recvr[...].astype(F32)
    level = part[:, :, :, 64:65] + part[:, :, :, 96:97] + part[:, :, :, 112:113]
    share = jnp.exp2(level - jnp.max(level, axis=1, keepdims=True))
    mixed = jnp.sum(part * share, axis=1) / jnp.sum(share, axis=1)
    both = jnp.where(low((32, 128)), mixed[0], swap(mixed[1]))
    sendf[...] = both.reshape(NX, 8, 128)

    def f_copy(n):
        t = at_x(n % NX)
        u = at_y(n // NX)
        return remote(sendf.at[t], aud.at[y, x], f_s.at[u, t], f_r.at[y, x], peer(z, t, c, u))

    loop(1, NX * ny, lambda n: f_copy(n).start())
    aud[y, x] = sendf[x]

    for copy in (a_copy, k_copy, v_copy, q_copy):
        for d in range(1, NX):
            copy(d).wait_send()
    for copy in (z_share, kv_share):
        copy.wait_send()

    def sent_ring(d):
        z_copy(d).wait_send()
        for m in range(2):
            r_copy(at_z(d), m).wait_send()

    loop(1, nz, sent_ring)
    r_copy(z, other).wait_send()
    loop(1, NX * ny, lambda n: o_copy(at_x(n % NX), n // NX).wait_send())

    def wait_o(n):
        t = at_x(n % NX)
        u = at_y(n // NX)
        arrived(attn.at[u, t], o_r.at[u, t])

    loop(1, NX * ny, wait_o)
    every = [(u, t) for u in range(ny) for t in range(NX)]
    local[6].wait()
    hidden = jnp.concatenate([attn[u, t] for u, t in every], axis=1)
    width = wv.shape[1] // 4
    for n in range(4):
        cols = pl.ds(n * width, width)
        vo[:, cols] = nn_dot(hidden, wv[:, cols]).astype(BF)

    def wait_f(n):
        t = at_x(n % NX)
        u = at_y(n // NX)
        arrived(aud.at[u, t], f_r.at[u, t])

    loop(1, NX * ny, wait_f)
    local[7].wait()
    hidden = jnp.concatenate([aud[u, t] for u, t in every], axis=1).astype(BF)
    ao[...] = nn_dot(hidden, wa[...]).astype(BF)

    loop(1, NX * ny, lambda n: f_copy(n).wait_send())


def write_out(v_in, a_in, v_out, a_out, sem):
    copies = [pltpu.make_async_copy(v_in, v_out, sem.at[0]), pltpu.make_async_copy(a_in, a_out, sem.at[1])]
    for copy in copies:
        copy.start()
    for copy in copies:
        copy.wait()


def per_device(nz, ny, vq, vk, vv, aq, ak, av, vl, al, wv, wa):
    rows, width = vq.shape
    a_rows = aq.shape[0]
    at = nz * 64
    vt = 2 * NX * 128
    hbm = pl.BlockSpec(memory_space=pl.ANY)
    smem = pl.BlockSpec(memory_space=pltpu.SMEM)
    vmem = pl.BlockSpec(memory_space=pltpu.VMEM)
    bf = lambda *shape: pltpu.VMEM(shape, BF)
    wide = lambda *shape: pltpu.VMEM(shape, F32)
    dma = lambda *shape: pltpu.SemaphoreType.DMA(shape)

    def body(*refs):
        kernel(nz, ny, *refs)

    made = pl.pallas_call(
        body,
        out_shape=(
            pltpu.VMEM((rows, wv.shape[1]), BF),
            pltpu.VMEM((a_rows, wa.shape[1]), BF),
        ),
        in_specs=[smem, smem] + [hbm] * 8,
        out_specs=(vmem, vmem),
        scratch_shapes=[
            bf(a_rows, width), bf(a_rows, width), bf(a_rows, width),
            bf(*wv.shape), bf(*wa.shape),
            bf(NX, 128, 128), bf(2, nz, 32, 128),
            bf(NX, 32, 128), bf(NX, 32, 128), bf(NX, 128, 128), bf(2, NX, 2, 128, 128),
            bf(2, nz, 96, 128),
            bf(2, 256, at), bf(2, 256, vt // 2), bf(at, 128), bf(at, 128), bf(vt, 128),
            bf(NX, 128, 128), bf(ny, NX, 128, 128),
            bf(2, nz, 32, 128), bf(2, nz, 32, 128),
            wide(NX, 8, 128), wide(ny, NX, 8, 128),
            dma(8),
            dma(NX), dma(NX), dma(NX), dma(NX), dma(2, NX), dma(2, NX),
            dma(nz), dma(nz), dma(2), dma(2), dma(2, nz), dma(2, nz),
            dma(ny, NX), dma(ny, NX), dma(ny, NX), dma(ny, NX),
        ],
        compiler_params=pltpu.CompilerParams(
            collective_id=0, has_side_effects=True, vmem_limit_bytes=56 * 1024 * 1024
        ),
        name="cross_attention",
    )(vl, al, vq, vk, vv, aq, ak, av, wv, wa)
    shapes = (jax.ShapeDtypeStruct((rows, wv.shape[1]), BF), jax.ShapeDtypeStruct((a_rows, wa.shape[1]), BF))
    return pl.pallas_call(
        write_out,
        out_shape=shapes,
        in_specs=[vmem, vmem],
        out_specs=(hbm, hbm),
        scratch_shapes=[dma(2)],
        name="write_out",
    )(*(pltpu.with_memory_space_constraint(m, pltpu.VMEM) for m in made))


def solution(mesh):
    nz = mesh.shape["seq"] // (2 * NX)
    ny = mesh.shape["head"]

    def program(*arrays):
        return per_device(nz, ny, *arrays)

    return jax.shard_map(
        program,
        mesh=mesh,
        in_specs=(*(P("seq", "head"),) * 6, P(), P(), P(None, "head"), P(None, "head")),
        out_specs=(P("seq", "head"), P("seq", "head")),
        check_vma=False,
    )
```

```python
import math

import jax
import jax.numpy as jnp
from jax import lax
from jax.experimental import pallas as pl
from jax.experimental.pallas import tpu as pltpu
from jax.sharding import PartitionSpec as P

HEAD_DIM = 64
NX = 4
VIDEO = [[[2]], [[0, 1], [3]]]
AUDIO = 2
MESH = pl.DeviceIdType.MESH
BF = jnp.bfloat16
F32 = jnp.float32
FORBID = -65536.0
LOG2E = math.log2(math.e)
SCALE = LOG2E / math.sqrt(HEAD_DIM)


def nn_dot(a, b):
    return lax.dot_general(a, b, (((1,), (0,)), ((), ())), preferred_element_type=F32)


def swap(x):
    return pltpu.roll(x, 64, x.ndim - 1)


def lanes(shape):
    return lax.broadcasted_iota(jnp.int32, shape, len(shape) - 1)


def low(shape):
    return lanes(shape) < 64


def kernel(
    nz, ny,
    vl, al, vq, vk, vv, aq, ak, av, wv_hbm, wa_hbm,
    vo, ao,
    ina_q, ina_k, ina_v, wv, wa,
    tok_aug, aud_aug,
    senda, recva, recvq, kvb, zall, ka, kv, v0, v1, vg,
    sendo, attn, sendr, recvr, sendf, aud,
    in_sem,
    a_s, a_r, q_s, q_r, kv_s, kv_r, z_s, z_r, c_s, c_r, r_s, r_r, o_s, o_r, f_s, f_r,
):
    s = lax.axis_index("seq")
    y = lax.axis_index("head")
    z = s // (2 * NX)
    x = lax.rem(s // 2, NX)
    c = lax.rem(s, 2)
    other = 1 - c
    at = nz * 64
    vt = 2 * NX * 128

    def loop(lo, hi, body):
        for i in range(lo, hi):
            body(i)

    def at_x(d):
        return lax.rem(x + d, NX)

    def at_z(d):
        return lax.rem(z + d, nz)

    def at_y(d):
        return lax.rem(y + d, ny)

    def peer(zz, xx, cc, yy):
        return ((zz * NX + xx) * 2 + cc, yy)

    def remote(src, dst, ss, rs, to):
        return pltpu.make_async_remote_copy(
            src_ref=src, dst_ref=dst, send_sem=ss, recv_sem=rs, device_id=to, device_id_type=MESH
        )

    partner = peer(z, x, other, y)

    def arrived(dst, rs):
        remote(dst, dst, rs, rs, partner).wait_recv()

    def columns(ref, t):
        return ref.at[:, pl.ds(pl.multiple_of(t * 128, 128), 128)]

    local = [
        pltpu.make_async_copy(src, dst, in_sem.at[i])
        for i, (src, dst) in enumerate(
            [
                (aq, ina_q), (ak, ina_k), (av, ina_v),
                (columns(vq, x), recvq.at[x]),
                (columns(vk, x), kvb.at[c, x, 0]),
                (columns(vv, x), kvb.at[c, x, 1]),
                (wv_hbm, wv), (wa_hbm, wa),
            ]
        )
    ]
    for copy in local[:6]:
        copy.start()

    barrier = pltpu.get_barrier_semaphore()

    def greet(to):
        pl.semaphore_signal(barrier, inc=1, device_id=to, device_id_type=MESH)

    for d in range(1, NX):
        greet(peer(z, at_x(d), c, y))
    for d in sorted(range(1, nz), key=lambda d: abs(d - nz // 2)):
        greet(peer(at_z(d), x, c, y))
    greet(partner)
    for d in range(1, ny):
        greet(peer(z, x, c, at_y(d)))

    v_end = [vl[0]]
    a_end = [al[0]]
    for i in range(1, 4):
        v_end.append(v_end[-1] + vl[i])
        a_end.append(a_end[-1] + al[i])

    def clip_of(pos, ends):
        total = jnp.zeros_like(pos)
        for e in ends:
            total = total + (pos >= e).astype(jnp.int32)
        return total

    def iotas(shape):
        return [lax.broadcasted_iota(jnp.int32, shape, i) for i in range(len(shape))]

    def audio_pos(core, slab, row):
        pos = slab * 64 + (row >> 3) * 16 + core * 8 + (row & 7) + at // 2
        return jnp.where(pos >= at, pos - at, pos)

    place, row, lane = iotas((NX, 128, 128))
    token = ((z * NX + place) * 2 + c) * 128 + row
    tok_aug[...] = jnp.where(clip_of(token, v_end) == lane, 1.0, 0.0).astype(BF)
    core, slab, row, lane = iotas((2, nz, 32, 128))
    forbidden = (lane < 4) & (clip_of(audio_pos(core, slab, row), a_end) != lane)
    aud_aug[...] = jnp.where(forbidden, FORBID, 0.0).astype(BF)
    mark, col = iotas((128, NX * 128))
    for m in range(2):
        token = (z * NX + (col >> 7)) * 256 + m * 128 + (col & 127)
        kv[m, 128:256] = jnp.where(clip_of(token, v_end) == mark, 1.0, 0.0).astype(BF)
    mark, col = iotas((128, nz * 32))
    for m in range(2):
        forbidden = (mark < 4) & (clip_of(audio_pos(m, col >> 5, col & 31), a_end) != mark)
        marks = jnp.where(forbidden, FORBID, 0.0).astype(BF)
        ka[m, 128:256] = jnp.concatenate([marks, marks], axis=1)
        ka[m, 0:128] = jnp.zeros((128, at), BF)

    for i in range(3):
        local[i].wait()
    for p in range(NX):
        cols = pl.ds(128 * p, 128)
        k8, v8, q8 = (r[:, cols].astype(F32) for r in (ina_k, ina_v, ina_q))
        senda[p] = jnp.concatenate([k8, v8, q8, q8], axis=0).astype(BF)

    pl.semaphore_wait(barrier, 1 + nz - 1 + NX - 1 + ny - 1)

    def a_copy(d):
        t = at_x(d)
        return remote(senda.at[t], recva.at[x], a_s.at[t], a_r.at[x], peer(z, t, c, y))

    def q_copy(d):
        t = at_x(d)
        return remote(columns(vq, t), recvq.at[x], q_s.at[t], q_r.at[x], peer(z, t, c, y))

    def k_copy(d):
        t = at_x(d)
        return remote(columns(vk, t), kvb.at[c, x, 0], kv_s.at[0, t], kv_r.at[0, x], peer(z, t, c, y))

    def v_copy(d):
        t = at_x(d)
        return remote(columns(vv, t), kvb.at[c, x, 1], kv_s.at[1, t], kv_r.at[1, x], peer(z, t, c, y))

    for copy in (a_copy, k_copy, v_copy, q_copy):
        for d in range(1, NX):
            copy(d).start()

    for copy in local[6:]:
        copy.start()
    recva[x] = senda[x]

    for d in range(1, NX):
        arrived(recva.at[at_x(d)], a_r.at[at_x(d)])
    got = recva[...].astype(F32)
    rows = [got[:, 8 * i : 8 * i + 8].reshape(32, 128) for i in range(3)]
    zall[c, z] = jnp.concatenate(rows, axis=0).astype(BF)

    def z_copy(d):
        t = at_z(d)
        return remote(zall.at[c, z], zall.at[c, z], z_s.at[t], z_r.at[z], peer(t, x, c, y))

    for d in sorted(range(1, nz), key=lambda d: abs(d - nz // 2)):
        z_copy(d).start()

    z_share = remote(zall.at[c], zall.at[c], c_s.at[0], c_r.at[0], partner)
    kv_share = remote(kvb.at[c], kvb.at[c], c_s.at[1], c_r.at[1], partner)
    for i in (4, 5):
        local[i].wait()
    for n in range(1, NX):
        for i in range(2):
            arrived(kvb.at[c, at_x(n), i], kv_r.at[i, at_x(n)])
    kv_share.start()
    low_row = low((1, 128))
    head0 = jnp.where(low_row, 1.0, 0.0).astype(BF)
    head1 = jnp.where(low_row, 0.0, 1.0).astype(BF)
    mine = jnp.where(c == 0, head0.astype(F32), head1.astype(F32)).astype(BF)
    rest = jnp.where(c == 0, head1.astype(F32), head0.astype(F32)).astype(BF)
    half_at = at // 2

    def prepare_audio(m):
        rows = pl.ds(pl.multiple_of(m * half_at, half_at), half_at)
        key = zall[m, :, 0:32].reshape(half_at, 128).T
        ka[m, 0:64, 0:half_at] = key[0:64]
        ka[m, 64:128, half_at:at] = key[64:128]
        value = zall[m, :, 32:64].reshape(half_at, 128)
        v0[rows] = value * head0 + head1
        v1[rows] = value * head1 + head0

    def prepare_video(m):
        rows = pl.ds(pl.multiple_of(m * (vt // 2), vt // 2), vt // 2)
        kv[m, 0:128] = kvb[m, :, 0].reshape(vt // 2, 128).T
        vg[rows] = kvb[m, :, 1].reshape(vt // 2, 128) * mine + rest

    prepare_video(c)
    for d in range(1, nz):
        arrived(zall.at[c, at_z(d)], z_r.at[at_z(d)])
    z_share.start()

    prepare_audio(c)
    local[3].wait()
    for d in range(1, NX):
        arrived(recvq.at[at_x(d)], q_r.at[at_x(d)])
    arrived(zall.at[other], c_r.at[0])
    prepare_audio(other)

    low128 = low((128, 128))

    def o_copy(t, e):
        u = at_y(e)
        return remote(sendo.at[t], attn.at[y, x], o_s.at[u, t], o_r.at[y, x], peer(z, t, c, u))

    def video_block(t):
        query = jnp.concatenate([recvq[t], tok_aug[t]], axis=1)
        scs = [nn_dot(query, ka[m]) for m in range(2)]
        outs = []
        for i, values in ((0, v0[...]), (1, v1[...])):
            half = jnp.concatenate([sc[:, i * half_at : (i + 1) * half_at] for sc in scs], axis=1)
            top = jnp.max(half, axis=1, keepdims=True)
            w = jnp.exp2((half - top) * SCALE).astype(BF)
            outs.append(nn_dot(w, values))
        num = jnp.where(low128, outs[0], outs[1])
        den = swap(jnp.where(low128, outs[1], outs[0]))
        return (num / den).astype(BF)

    def video_steps(ds):
        done = [video_block(at_x(d)) for d in ds]
        for d, block in zip(ds, done):
            sendo[at_x(d)] = block
        for d in ds:
            for e in sorted(range(0 if d else 1, ny), key=lambda e: abs(e - ny // 2)):
                o_copy(at_x(d), e).start()

    lane128 = lanes((128, 128))

    def audio_block(p):
        query = zall[:, pl.ds(2 * p, 2), 64:96].reshape(128, 128) * mine
        query = jnp.concatenate([query, aud_aug[:, pl.ds(2 * p, 2)].reshape(128, 128)], axis=1)
        sc = jnp.concatenate([nn_dot(query, kv[m]) for m in range(2)], axis=1)
        top = jnp.max(sc, axis=1, keepdims=True)
        w = jnp.exp2((sc - top) * SCALE).astype(BF)
        full = nn_dot(w, vg[...])
        turned = swap(full)
        full, turned = jnp.where(c == 0, full, turned), jnp.where(c == 0, turned, full)
        mean = full / turned
        level = top * SCALE + jnp.log(jnp.where(low128, 1.0, full)) * LOG2E
        first = level.astype(BF).astype(F32)
        second = (level - first).astype(BF).astype(F32)
        third = level - first - second
        parts = jnp.where(lane128 < 96, first, jnp.where(lane128 < 112, second, third))
        return jnp.where(low128, mean, parts).reshape(2, 2, 32, 128).astype(BF)

    def r_copy(t, m):
        return remote(sendr.at[m, t], recvr.at[c, z], r_s.at[m, t], r_r.at[c, z], peer(t, x, m, y))

    def audio_steps(ds):
        ps = [lax.rem(z // 2 + d, nz // 2) for d in ds]
        done = [audio_block(p) for p in ps]
        for p, blocks in zip(ps, done):
            sendr[:, pl.ds(2 * p, 2)] = blocks
        for d, p in zip(ds, ps):
            for m in range(2):
                if d:
                    for i in range(2):
                        r_copy(2 * p + i, m).start()
                else:
                    r_copy(2 * p + 1 - lax.rem(z, 2), m).start()
            if d == 0:
                r_copy(z, other).start()

    pairs = sorted(range(1, nz // 2), key=lambda d: abs(d - nz // 4)) + [0]
    for ds in VIDEO[0]:
        video_steps(ds)
    arrived(kvb.at[other], c_r.at[1])
    prepare_video(other)
    for i in range(0, len(pairs), AUDIO):
        audio_steps(pairs[i : i + AUDIO])
    recvr[c, z] = sendr[c, z]
    for ds in VIDEO[1]:
        video_steps(ds)
    attn[y, x] = sendo[x]

    arrived(recvr.at[other, z], r_r.at[other, z])
    for d in range(1, nz):
        for m in range(2):
            arrived(recvr.at[m, at_z(d)], r_r.at[m, at_z(d)])
    part = recvr[...].astype(F32)
    level = part[:, :, :, 64:65] + part[:, :, :, 96:97] + part[:, :, :, 112:113]
    share = jnp.exp2(level - jnp.max(level, axis=1, keepdims=True))
    mixed = jnp.sum(part * share, axis=1) / jnp.sum(share, axis=1)
    both = jnp.where(low((32, 128)), mixed[0], swap(mixed[1]))
    sendf[...] = both.reshape(NX, 8, 128)

    def f_copy(n):
        t = at_x(n % NX)
        u = at_y(n // NX)
        return remote(sendf.at[t], aud.at[y, x], f_s.at[u, t], f_r.at[y, x], peer(z, t, c, u))

    loop(1, NX * ny, lambda n: f_copy(n).start())
    aud[y, x] = sendf[x]

    for copy in (a_copy, k_copy, v_copy, q_copy):
        for d in range(1, NX):
            copy(d).wait_send()
    for copy in (z_share, kv_share):
        copy.wait_send()

    def sent_ring(d):
        z_copy(d).wait_send()
        for m in range(2):
            r_copy(at_z(d), m).wait_send()

    loop(1, nz, sent_ring)
    r_copy(z, other).wait_send()
    loop(1, NX * ny, lambda n: o_copy(at_x(n % NX), n // NX).wait_send())

    def wait_o(n):
        t = at_x(n % NX)
        u = at_y(n // NX)
        arrived(attn.at[u, t], o_r.at[u, t])

    loop(1, NX * ny, wait_o)
    every = [(u, t) for u in range(ny) for t in range(NX)]
    local[6].wait()
    hidden = jnp.concatenate([attn[u, t] for u, t in every], axis=1)
    width = wv.shape[1] // 4
    for n in range(4):
        cols = pl.ds(n * width, width)
        vo[:, cols] = nn_dot(hidden, wv[:, cols]).astype(BF)

    def wait_f(n):
        t = at_x(n % NX)
        u = at_y(n // NX)
        arrived(aud.at[u, t], f_r.at[u, t])

    loop(1, NX * ny, wait_f)
    local[7].wait()
    hidden = jnp.concatenate([aud[u, t] for u, t in every], axis=1).astype(BF)
    ao[...] = nn_dot(hidden, wa[...]).astype(BF)

    loop(1, NX * ny, lambda n: f_copy(n).wait_send())


def write_out(v_in, a_in, v_out, a_out, sem):
    copies = [pltpu.make_async_copy(v_in, v_out, sem.at[0]), pltpu.make_async_copy(a_in, a_out, sem.at[1])]
    for copy in copies:
        copy.start()
    for copy in copies:
        copy.wait()


def per_device(nz, ny, vq, vk, vv, aq, ak, av, vl, al, wv, wa):
    rows, width = vq.shape
    a_rows = aq.shape[0]
    at = nz * 64
    vt = 2 * NX * 128
    hbm = pl.BlockSpec(memory_space=pl.ANY)
    smem = pl.BlockSpec(memory_space=pltpu.SMEM)
    vmem = pl.BlockSpec(memory_space=pltpu.VMEM)
    bf = lambda *shape: pltpu.VMEM(shape, BF)
    wide = lambda *shape: pltpu.VMEM(shape, F32)
    dma = lambda *shape: pltpu.SemaphoreType.DMA(shape)

    def body(*refs):
        kernel(nz, ny, *refs)

    made = pl.pallas_call(
        body,
        out_shape=(
            pltpu.VMEM((rows, wv.shape[1]), BF),
            pltpu.VMEM((a_rows, wa.shape[1]), BF),
        ),
        in_specs=[smem, smem] + [hbm] * 8,
        out_specs=(vmem, vmem),
        scratch_shapes=[
            bf(a_rows, width), bf(a_rows, width), bf(a_rows, width),
            bf(*wv.shape), bf(*wa.shape),
            bf(NX, 128, 128), bf(2, nz, 32, 128),
            bf(NX, 32, 128), bf(NX, 32, 128), bf(NX, 128, 128), bf(2, NX, 2, 128, 128),
            bf(2, nz, 96, 128),
            bf(2, 256, at), bf(2, 256, vt // 2), bf(at, 128), bf(at, 128), bf(vt, 128),
            bf(NX, 128, 128), bf(ny, NX, 128, 128),
            bf(2, nz, 32, 128), bf(2, nz, 32, 128),
            wide(NX, 8, 128), wide(ny, NX, 8, 128),
            dma(8),
            dma(NX), dma(NX), dma(NX), dma(NX), dma(2, NX), dma(2, NX),
            dma(nz), dma(nz), dma(2), dma(2), dma(2, nz), dma(2, nz),
            dma(ny, NX), dma(ny, NX), dma(ny, NX), dma(ny, NX),
        ],
        compiler_params=pltpu.CompilerParams(
            collective_id=0, has_side_effects=True, vmem_limit_bytes=56 * 1024 * 1024
        ),
        name="cross_attention",
    )(vl, al, vq, vk, vv, aq, ak, av, wv, wa)
    shapes = (jax.ShapeDtypeStruct((rows, wv.shape[1]), BF), jax.ShapeDtypeStruct((a_rows, wa.shape[1]), BF))
    return pl.pallas_call(
        write_out,
        out_shape=shapes,
        in_specs=[vmem, vmem],
        out_specs=(hbm, hbm),
        scratch_shapes=[dma(2)],
        name="write_out",
    )(*(pltpu.with_memory_space_constraint(m, pltpu.VMEM) for m in made))


def solution(mesh):
    nz = mesh.shape["seq"] // (2 * NX)
    ny = mesh.shape["head"]

    def program(*arrays):
        return per_device(nz, ny, *arrays)

    return jax.shard_map(
        program,
        mesh=mesh,
        in_specs=(*(P("seq", "head"),) * 6, P(), P(), P(None, "head"), P(None, "head")),
        out_specs=(P("seq", "head"), P("seq", "head")),
        check_vma=False,
    )
```
